128 devices in a mesh: replica: 16 (over z_hi, y, core), shard: 8 (over x, z_lo).
Axes of the slice: x: 4, y: 4, z: 4 (z_hi: 2, z_lo: 2; z = z_hi * 2 + z_lo), core: 2. Of those that a mesh axis runs over, the one named last changes fastest.
Arguments:
- hidden_in: bfloat16 [32768, 1024], P(('replica', 'shard')), may hold values from -6 to 6
- segments: int32 [32768], P(('replica', 'shard')), may hold values from 0 to 4, as said below
- out_grad: bfloat16 [32768, 1024], P(('replica', 'shard')), may hold values from -6 to 6
- w_qkv: bfloat16 [1024, 3072], P('shard'), may hold values from -0.1875 to 0.1875
- w_out: bfloat16 [1024, 1024], P('shard'), may hold values from -0.75 to 0.75
- w_up: bfloat16 [1024, 4096], P('shard'), may hold values from -0.1875 to 0.1875
- w_down: bfloat16 [4096, 1024], P('shard'), may hold values from -0.09375 to 0.09375
- norm_gains: bfloat16 [2, 1024], P(None, 'shard'), may hold values from 0.5 to 1.5
- bias_rows: bfloat16 [6, 1024], P(None, 'shard'), may hold values from -1 to 1
- up_bias: bfloat16 [4096], P('shard'), may hold values from -1 to 1
Outputs:
- hidden_out: bfloat16 [32768, 1024], P(('replica', 'shard'))
- in_grad: float32 [32768, 1024], P(('replica', 'shard'))
- grad_qkv: float32 [1024, 3072], P('shard')
- grad_out: float32 [1024, 1024], P('shard')
- grad_up: float32 [1024, 4096], P('shard')
- grad_down: float32 [4096, 1024], P('shard')
- grad_gains: float32 [2, 1024], P(None, 'shard')
- grad_biases: float32 [6, 1024], P(None, 'shard')
- grad_up_bias: float32 [4096], P('shard')
The draws below stay inside these ranges and needn't reach their ends.
Inputs may be any that keep to these rules, and one draw needn't show every extreme that they name: `segments`: segment numbers start at 0 and never fall along each pack of 2048 tokens; every pack holds five documents; in every pack one document starts within the first 256 tokens and ends within the last 256.
All inputs are finite; a program needn't handle non-finite values.
Results may differ from the reference program's by a relative error of at most 0.024.
Values may be sent and summed in bfloat16 or wider, within the bound.
No kernel may reach another device: no remote copies, remote signals or barrier semaphores. Data moves between devices by JAX's collectives and lax.ppermute only.
A program may use at most 192 MiB of HBM per device.

```python
import jax
import jax.numpy as jnp
from jax import lax

D = 1024
H = 16
HD = 64
FF = 4096
TOK_DEV = 256
SEQ = 2048
PACKS = 16
TOKENS = 32768


def draw_segments(key, part):
    key = jax.random.fold_in(key, 7)
    key_first, key_head, key_last, key_tail = jax.random.split(key, 4)
    half = max(TOK_DEV // 2, 2)
    first = jax.random.randint(key_first, (PACKS,), 2, half + 1)
    head = jax.random.randint(key_head, (PACKS,), 1, first)
    last = SEQ - jax.random.randint(key_last, (PACKS,), 2, half + 1)
    tail = last + jax.random.randint(key_tail, (PACKS,), 1, SEQ - last)
    position = jnp.arange(SEQ, dtype=jnp.int32)[None, :]
    flags = (position == head[:, None]) | (position == first[:, None]) | (position == last[:, None]) | (position == tail[:, None])
    numbers = jnp.cumsum(flags.astype(jnp.int32), axis=1)
    return numbers.reshape(TOKENS).astype(jnp.int32)


def steps_of(key, shape, pieces, least, top_value):
    def one(dim, blocks):
        heights = jax.random.uniform(jax.random.fold_in(jax.random.fold_in(key, 6), dim), (blocks,), jnp.float32, least / len(pieces), top_value / len(pieces))
        return jnp.repeat(jnp.exp(heights), shape[dim] // blocks).reshape((-1,) + (1,) * (len(shape) - dim - 1))

    level = one(*pieces[0])
    for cut in pieces[1:]:
        level = level * one(*cut)
    return level


def noise(rng, dims, scale, most, cuts=(), held_as=jnp.bfloat16):
    drawn = scale * jax.random.normal(rng, dims, jnp.float32)
    if cuts:
        drawn = drawn * steps_of(rng, dims, cuts, -0.22, 0.18)
    return jnp.clip(drawn, -most, most).astype(held_as)


def setup_inputs(seed: int = 0) -> dict:
    splits = jax.random.split(jax.random.key(seed), 11)
    return {
        "hidden_in": noise(splits[0], (TOKENS, D), 1.0, 6.0, ((0, 128),)),
        "segments": draw_segments(jax.random.fold_in(splits[10], 71), 0),
        "out_grad": noise(splits[2], (TOKENS, D), 1.0, 6.0, ((0, 128),)),
        "w_qkv": noise(splits[3], (D, 3 * D), D ** -0.5, 0.1875, ((0, 8),)),
        "w_out": noise(splits[4], (D, D), (D // 16) ** -0.5, 0.75, ((0, 8),)),
        "w_up": noise(splits[5], (D, FF), D ** -0.5, 0.1875, ((0, 8),)),
        "w_down": noise(splits[6], (FF, D), FF ** -0.5, 0.09375, ((0, 8),)),
        "norm_gains": jnp.clip(1.0 + 0.1 * jax.random.normal(splits[7], (2, D), jnp.float32), 0.5, 1.5).astype(jnp.bfloat16),
        "bias_rows": noise(splits[8], (6, D), 0.2, 1.0, ((1, 8),)),
        "up_bias": noise(splits[9], (FF,), 0.2, 1.0, ((0, 8),)),
    }


@jax.custom_vjp
def low(v):
    return lax.optimization_barrier(v.astype(jnp.bfloat16)).astype(jnp.float32)

@jax.custom_vjp
def low_back(v):
    return v

def low_keep(v):
    return (low(v), None)

def low_pass(kept, grad):
    return (grad,)

def back_keep(v):
    return (v, None)

def back_low(kept, grad):
    return (low(grad),)
low.defvjp(low_keep, low_pass)
low_back.defvjp(back_keep, back_low)
highest = lax.Precision.HIGHEST

def layer_norm(values, gain, shift):
    center = values - lax.optimization_barrier(jnp.mean(values, axis=-1, keepdims=True))
    spread = lax.optimization_barrier(jnp.mean(center * center, axis=-1, keepdims=True))
    return center * lax.rsqrt(spread + 1e-05) * gain + shift

def attention(queries, keys, values, seg):
    rows_block = min(512, SEQ)
    count = SEQ // rows_block
    scale = HD ** (-0.5)
    slopes = jnp.exp2(-8.0 * (jnp.arange(H) + 1).astype(jnp.float32) / H) * (2.0 / TOK_DEV)
    key_pos = jnp.arange(SEQ, dtype=jnp.int32)

    def one_block(start):
        query_rows = lax.dynamic_slice_in_dim(queries, start, rows_block, 0)
        query_seg = lax.dynamic_slice_in_dim(seg, start, rows_block, 0)
        raw = jnp.einsum('qhd,khd->hqk', query_rows, keys, precision=highest) * scale
        raw = low_back(raw)
        distance = (start + jnp.arange(rows_block, dtype=jnp.int32))[:, None] - key_pos[None, :]
        allowed = (query_seg[:, None] == seg[None, :]) & (distance >= 0)
        scores = raw - slopes[:, None, None] * distance.astype(jnp.float32)[None]
        scores = jnp.where(allowed[None], scores, -1e+30)
        probs = low(jax.nn.softmax(scores, axis=-1))
        return jnp.einsum('hqk,khd->qhd', probs, values, precision=highest)
    starts = jnp.arange(count, dtype=jnp.int32) * rows_block
    blocks = lax.map(jax.checkpoint(one_block), starts)
    return blocks.reshape(SEQ, H * HD)

def forward(params, rows_in, seg):
    w_qkv, w_out, w_up, w_down, gains, biases, up_bias = params
    normed = low(layer_norm(rows_in, gains[0], biases[0]))
    zero_row = jnp.zeros_like(biases[1])
    mixed = jnp.dot(normed, w_qkv, precision=highest) + jnp.concatenate([biases[1], zero_row, biases[2]])
    mixed = low_back(low(mixed))
    queries = mixed[:, :D].reshape(SEQ, H, HD)
    keys = mixed[:, D:2 * D].reshape(SEQ, H, HD)
    values = mixed[:, 2 * D:].reshape(SEQ, H, HD)
    context = low_back(low(attention(queries, keys, values, seg)))
    branch = low_back(jnp.dot(context, w_out, precision=highest) + biases[3])
    middle = rows_in + branch
    second = low(layer_norm(middle, gains[1], biases[4]))
    before = low_back(jnp.dot(second, w_up, precision=highest) + up_bias)
    after = low(jax.nn.gelu(before, approximate=True))
    return middle + low_back(jnp.dot(after, w_down, precision=highest) + biases[5])

def reference(hidden_in, segments, out_grad, w_qkv, w_out, w_up, w_down, norm_gains, bias_rows, up_bias):
    params = (w_qkv.astype(jnp.float32), w_out.astype(jnp.float32), w_up.astype(jnp.float32), w_down.astype(jnp.float32), norm_gains.astype(jnp.float32), bias_rows.astype(jnp.float32), up_bias.astype(jnp.float32))
    inputs = hidden_in.astype(jnp.float32).reshape(PACKS, SEQ, D)
    cotangents = out_grad.astype(jnp.float32).reshape(PACKS, SEQ, D)
    seg_packs = segments.reshape(PACKS, SEQ)

    def one_pack(totals, item):
        rows_in, seg, cotangent = item
        outputs, pull = jax.vjp(lambda weights, inner: forward(weights, inner, seg), params, rows_in)
        grads, row_grad = pull(cotangent)
        totals = jax.tree.map(lambda left, right: left + right, totals, grads)
        return (totals, (outputs.astype(jnp.bfloat16), row_grad))
    start_totals = jax.tree.map(jnp.zeros_like, params)
    totals, (outputs, in_grads) = lax.scan(one_pack, start_totals, (inputs, seg_packs, cotangents))
    return (outputs.reshape(TOKENS, D), in_grads.reshape(TOKENS, D), totals[0], totals[1], totals[2], totals[3], totals[4], totals[5], totals[6])
```

```python
import functools

import jax
import jax.numpy as jnp
import numpy as np
from jax import lax
from jax.experimental import pallas as pl
from jax.experimental.pallas import tpu as pltpu
from jax.sharding import PartitionSpec as P

f32 = jnp.float32
bf16 = jnp.bfloat16

D = 1024
H = 16
HD = 64
TOK = 256
SEQ = 2048
NX, NZ, NY = 4, 2, 4
FWD_ROWS = 1024
BWD_ROWS = 512
FAR = -1e30

SLOPES = (2.0 ** (-8.0 * (np.arange(H) + 1) / H) / 128).astype(np.float32)


def nt(a, b):
    return lax.dot_general(a, b, (((1,), (1,)), ((), ())), preferred_element_type=f32)


def nn(a, b):
    return lax.dot_general(a, b, (((1,), (0,)), ((), ())), preferred_element_type=f32)


def tn(a, b):
    return lax.dot_general(a, b, (((0,), (0,)), ((), ())), preferred_element_type=f32)


def pieces(x):
    a = x.astype(bf16).astype(f32)
    r = x - a
    b = r.astype(bf16).astype(f32)
    return a, b, r - b


def lane_of(rows):
    return lax.broadcasted_iota(jnp.int32, (rows, 128), 1)


def key_features(seg_col, rows):
    feat = lane_of(rows) & 63
    pos = lax.broadcasted_iota(jnp.int32, (rows, 128), 0)
    coarse = (pos & -256).astype(f32)
    fine = (pos & 255).astype(f32)
    flag = (seg_col.astype(f32) == (feat - 9).astype(f32)).astype(f32)
    out = jnp.where(feat < 3, coarse, jnp.where(feat < 6, fine, jnp.where(feat < 9, 1.0, flag)))
    return jnp.where(feat < 14, out, 0.0).astype(bf16)


def fwd_kernel(bq, q_ref, k_ref, v_ref, seg_ref, segq_ref, slope_ref, c_ref, low_ref, qb_ref, k_s, vt_s, q_s):
    i = pl.program_id(0)

    @pl.when(i == 0)
    def _():
        feats = key_features(seg_ref[...], SEQ)
        left = lane_of(SEQ) < 64
        k_s[0] = jnp.where(left, k_ref[...], feats)
        k_s[1] = jnp.where(left, feats, k_ref[...])
        vt = v_ref[...].T
        for h in range(2):
            vt_s[h, 0:64, :] = vt[64 * h : 64 * h + 64]
            vt_s[h, 64:80, :] = jnp.ones((16, SEQ), bf16)

    lane = lane_of(bq)
    feat = lane & 63
    left = lane < 64
    off = jnp.where(segq_ref[...].astype(f32) == (feat - 9).astype(f32), 0.0, FAR)
    base = jnp.where(feat < 9, slope_ref[0:1, :], jnp.where(feat < 14, off, 0.0))
    q = q_ref[...].astype(f32) * (HD**-0.5)
    q_s[0] = jnp.where(left, q, base).astype(bf16)
    q_s[1] = jnp.where(left, base, q).astype(bf16)

    def tile(j, carry, diag):
        out = []
        for h in range(2):
            top, acc = carry[h]
            s = nt(k_s[h, pl.ds(pl.multiple_of(j * bq, bq), bq), :], q_s[h])
            if diag:
                kk = lax.broadcasted_iota(jnp.int32, (bq, bq), 0)
                qq = lax.broadcasted_iota(jnp.int32, (bq, bq), 1)
                s = jnp.where(kk <= qq, s, FAR)
            new = jnp.maximum(top, jnp.max(s, axis=0, keepdims=True))
            p = jnp.exp(s - new).astype(bf16)
            o = nn(vt_s[h, :, pl.ds(pl.multiple_of(j * bq, bq), bq)], p)
            out.append((new, acc * jnp.exp(top - new) + o))
        return tuple(out)

    init = tuple((jnp.full((1, bq), FAR, f32), jnp.zeros((80, bq), f32)) for _ in range(2))
    carry = tile(i, init, True)
    carry = lax.fori_loop(0, i, lambda j, c: tile(j, c, False), carry)
    outs = []
    rows = lax.broadcasted_iota(jnp.int32, (128, bq), 0)
    spread = jnp.zeros((128, bq), f32)
    for h in range(2):
        top, acc = carry[h]
        total = acc[64:65]
        outs.append(acc[:64] / total)
        for n, part in enumerate(pieces(-(top + jnp.log(total)))):
            spread = jnp.where(rows == 64 * (1 - h) + 6 + n, part, spread)
    ctx = jnp.concatenate(outs, axis=0).T
    c_ref[...] = ctx
    low_ref[...] = ctx.astype(bf16)
    full = base + spread.T
    qb_ref[0] = jnp.where(left, q, full).astype(bf16)
    qb_ref[1] = jnp.where(left, full, q).astype(bf16)


def attn_fwd(q, k, v, seg_col, slopes):
    bq = FWD_ROWS
    whole = pl.BlockSpec((SEQ, 128), lambda i: (0, 0))
    block = pl.BlockSpec((bq, 128), lambda i: (i, 0))
    return pl.pallas_call(
        functools.partial(fwd_kernel, bq),
        grid=(SEQ // bq,),
        in_specs=[
            block,
            whole,
            whole,
            pl.BlockSpec((SEQ, 1), lambda i: (0, 0)),
            pl.BlockSpec((bq, 1), lambda i: (i, 0)),
            pl.BlockSpec((8, 128), lambda i: (0, 0)),
        ],
        out_specs=[block, block, pl.BlockSpec((2, bq, 128), lambda i: (0, i, 0))],
        out_shape=[
            jax.ShapeDtypeStruct((SEQ, 128), f32),
            jax.ShapeDtypeStruct((SEQ, 128), bf16),
            jax.ShapeDtypeStruct((2, SEQ, 128), bf16),
        ],
        scratch_shapes=[
            pltpu.VMEM((2, SEQ, 128), bf16),
            pltpu.VMEM((2, 80, SEQ), bf16),
            pltpu.VMEM((2, bq, 128), bf16),
        ],
        compiler_params=pltpu.CompilerParams(vmem_limit_bytes=48 * 2**20),
        cost_estimate=pl.CostEstimate(flops=2 * 10**9, bytes_accessed=4 * 2**20, transcendentals=5 * 10**6),
        name="attn_fwd",
    )(q, k, v, seg_col, seg_col, slopes)


def bwd_kernel(bq, q_ref, k_ref, v_ref, d_ref, c_ref, seg_ref, dq_ref, dk_ref, dv_ref, k_s, v_s, kt_s, d_s, dk_acc, dv_acc):
    i = pl.program_id(0)
    n = pl.num_programs(0)

    @pl.when(i == 0)
    def _():
        feats = key_features(seg_ref[...], SEQ)
        left = lane_of(SEQ) < 64
        k_s[0] = jnp.where(left, k_ref[...], feats)
        k_s[1] = jnp.where(left, feats, k_ref[...])
        v_s[0] = jnp.where(left, v_ref[...], feats)
        v_s[1] = jnp.where(left, feats, v_ref[...])
        kt_s[...] = k_ref[...].T

    lane = lane_of(bq)
    feat = lane & 63
    left = lane < 64
    grad = d_ref[...].astype(f32)
    prod = grad * c_ref[...]
    for h in range(2):
        mine = left if h == 0 else ~left
        a, b, c = pieces(-jnp.sum(jnp.where(mine, prod, 0.0), axis=1, keepdims=True))
        extra = jnp.where(feat == 6, a, jnp.where(feat == 7, b, jnp.where(feat == 8, c, 0.0)))
        d_s[h] = jnp.where(mine, grad, extra).astype(bf16)

    def tile(j, carry, diag):
        out = []
        rows = pl.ds(pl.multiple_of(j * bq, bq), bq)
        for h in range(2):
            s = nt(k_s[h, rows, :], q_ref[h])
            if diag:
                kk = lax.broadcasted_iota(jnp.int32, (bq, bq), 0)
                qq = lax.broadcasted_iota(jnp.int32, (bq, bq), 1)
                s = jnp.where(kk <= qq, s, FAR)
            p = jnp.exp(s)
            ds = (p * nt(v_s[h, rows, :], d_s[h])).astype(bf16)
            dv = nn(p.astype(bf16), d_s[h])
            dk = nn(ds, q_ref[h])
            if diag:
                dv_acc[h, rows, :] = dv
                dk_acc[h, rows, :] = dk
            else:
                dv_acc[h, rows, :] += dv
                dk_acc[h, rows, :] += dk
            out.append(carry[h] + nn(kt_s[64 * h : 64 * h + 64, rows], ds))
        return tuple(out)

    init = tuple(jnp.zeros((64, bq), f32) for _ in range(2))
    carry = tile(i, init, True)
    carry = lax.fori_loop(0, i, lambda j, c: tile(j, c, False), carry)
    dq_ref[...] = (jnp.concatenate(carry, axis=0) * (HD**-0.5)).T.astype(bf16)

    @pl.when(i == n - 1)
    def _():
        side = lane_of(SEQ) < 64
        dk_ref[...] = jnp.where(side, dk_acc[0], dk_acc[1]).astype(bf16)
        dv_ref[...] = jnp.where(side, dv_acc[0], dv_acc[1]).astype(bf16)


def attn_bwd(qb, k, v, d, ctx, seg_col):
    bq = BWD_ROWS
    whole = pl.BlockSpec((SEQ, 128), lambda i: (0, 0))
    block = pl.BlockSpec((bq, 128), lambda i: (i, 0))
    return pl.pallas_call(
        functools.partial(bwd_kernel, bq),
        grid=(SEQ // bq,),
        in_specs=[
            pl.BlockSpec((2, bq, 128), lambda i: (0, i, 0)),
            whole,
            whole,
            block,
            block,
            pl.BlockSpec((SEQ, 1), lambda i: (0, 0)),
        ],
        out_specs=[block, whole, whole],
        out_shape=[jax.ShapeDtypeStruct((SEQ, 128), bf16)] * 3,
        scratch_shapes=[
            pltpu.VMEM((2, SEQ, 128), bf16),
            pltpu.VMEM((2, SEQ, 128), bf16),
            pltpu.VMEM((128, SEQ), bf16),
            pltpu.VMEM((2, bq, 128), bf16),
            pltpu.VMEM((2, SEQ, 128), f32),
            pltpu.VMEM((2, SEQ, 128), f32),
        ],
        compiler_params=pltpu.CompilerParams(vmem_limit_bytes=48 * 2**20),
        cost_estimate=pl.CostEstimate(flops=5 * 10**9, bytes_accessed=6 * 2**20, transcendentals=5 * 10**6),
        name="attn_bwd",
    )(qb, k, v, d, ctx, seg_col)


def place(zh, y, c, x, zl):
    return ((zh * NY + y) * 2 + c) * 8 + x * NZ + zl


def take_from(array, dx=0, dz=0, dy=0, dc=0, dh=0):
    pairs = []
    for zh in range(2):
        for y in range(NY):
            for c in range(2):
                for x in range(NX):
                    for zl in range(NZ):
                        src = place((zh + dh) % 2, (y + dy) % NY, (c + dc) % 2, (x + dx) % NX, (zl + dz) % NZ)
                        pairs.append((src, place(zh, y, c, x, zl)))
    return lax.ppermute(array, ("replica", "shard"), pairs)


def piece(array, index, size, axis):
    return lax.dynamic_slice_in_dim(array, index * size, size, axis)


def put(target, value, index, axis):
    starts = [0] * target.ndim
    starts[axis] = index
    return lax.dynamic_update_slice(target, value.astype(target.dtype), starts)


def from_partner(array, axis, core):
    half = array.shape[axis] // 2
    mine = take_from(piece(array, core, half, axis), dz=1)
    other = take_from(mine, dc=1)
    out = jnp.zeros_like(array)
    return put(put(out, mine, core * half, axis), other, (1 - core) * half, axis)


def add_low(*parts):
    total = parts[0].astype(f32)
    for part in parts[1:]:
        total = total + part.astype(f32)
    return total.astype(bf16)


def spread_x(parts):
    return [parts[0]] + [take_from(parts[r], dx=-r) for r in range(1, NX)]


def gather_x(block):
    return [block] + [take_from(block, dx=r) for r in range(1, NX)]


def layer_norm(values, gain, shift):
    center = values - jnp.mean(values, axis=-1, keepdims=True)
    spread = jnp.mean(center * center, axis=-1, keepdims=True)
    return center * lax.rsqrt(spread + 1e-05) * gain + shift


def reduce_core_y(array, core, y):
    kept = piece(array, core, 64, 2)
    held = add_low(kept, take_from(piece(array, 1 - core, 64, 2), dc=1))
    return held


def reduce_y(held, y):
    own = piece(held, y, 16, 2)
    come = [take_from(piece(held, (y + r) % NY, 16, 2), dy=-r) for r in range(1, NY)]
    return add_low(own, *come)


def reduce_z(held, zl):
    own = jnp.squeeze(piece(held, zl, 1, 1), 1)
    come = take_from(jnp.squeeze(piece(held, 1 - zl, 1, 1), 1), dz=1)
    half = add_low(own, come)
    return add_low(half, take_from(half, dh=1))


def to_owner_x(part, x):
    out = jnp.zeros_like(part)
    for r in range(NX):
        block = lax.dynamic_index_in_dim(part, (x + r) % NX, 0, keepdims=True)
        got = block if r == 0 else take_from(block, dx=-r)
        out = put(out, got, (x - r) % NX, 0)
    return out


def gather_y_core(part, y, core):
    n, rows, cols = part.shape
    four = jnp.zeros((n, NY, rows, cols), bf16)
    for r in range(NY):
        got = part if r == 0 else take_from(part, dy=r)
        four = put(four, got[:, None], (y + r) % NY, 1)
    out = jnp.zeros((n, 2, NY, rows, cols), bf16)
    out = put(out, four[:, None], core, 1)
    return put(out, take_from(four, dc=1)[:, None], 1 - core, 1)


def per_device(hidden_in, segments, out_grad, w_qkv, w_out, w_up, w_down, norm_gains, bias_rows, up_bias):
    replica = lax.axis_index("replica")
    shard = lax.axis_index("shard")
    core = replica % 2
    y = (replica // 2) % NY
    x = shard // NZ
    zl = shard % NZ

    pack = jnp.concatenate(
        [
            norm_gains,
            bias_rows,
            up_bias.reshape(4, 128),
            segments.astype(bf16).reshape(2, 128),
            jnp.zeros((2, 128), bf16),
        ]
    )
    packs = lax.all_to_all(jnp.broadcast_to(pack[None], (8, 16, 128)), "shard", 0, 0)
    wide = packs.transpose(1, 0, 2).reshape(16, D).astype(f32)
    gains = wide[0:2]
    biases = wide[2:8]
    up_row = lax.dynamic_slice(packs[:, 8:12].reshape(NX, D), (x, 0), (1, D)).astype(f32)
    seg_all = packs[:, 12:14].reshape(SEQ)
    seg_col = seg_all.astype(f32).reshape(SEQ, 1)

    full_out = lax.all_gather(w_out, "shard", axis=0, tiled=True)

    rows_in = hidden_in.astype(f32)
    normed_f, first_pull = jax.vjp(layer_norm, rows_in, gains[0], biases[0])
    normed = normed_f.astype(bf16)

    def columns(weight, groups, size):
        parts = weight.reshape(128, groups, NX, size)
        send = [
            lax.dynamic_index_in_dim(parts, (x + r) % NX, 2, keepdims=False).reshape(1, 128, groups * size)
            for r in range(NX)
        ]
        come = spread_x(send)
        held = jnp.zeros((NX, 128, groups * size), bf16)
        for r in range(NX):
            held = put(held, come[r], (x - r) % NX, 0)
        other = from_partner(held, 1, core)
        out = jnp.zeros((NX, NZ, 128, groups * size), bf16)
        out = put(put(out, held[:, None], zl, 1), other[:, None], 1 - zl, 1)
        return out.reshape(D, groups * size)

    qkv_x = columns(w_qkv, 3, 256)
    normed_blocks = gather_x(normed)
    normed_all = jnp.zeros((NX, TOK, D), bf16)
    for r in range(NX):
        normed_all = put(normed_all, normed_blocks[r][None], (x + r) % NX, 0)
    normed_all = normed_all.reshape(NX * TOK, D)
    grad_blocks = gather_x(out_grad)
    up_x = columns(w_up, 1, D)
    down_other = from_partner(w_down, 0, core)
    down_x = jnp.zeros((NZ, 512, D), bf16)
    down_x = put(put(down_x, w_down[None], zl, 0), down_other[None], 1 - zl, 0).reshape(D, D)

    bias_q = lax.dynamic_slice(biases[1], (x * 256,), (256,))
    bias_v = lax.dynamic_slice(biases[2], (x * 256,), (256,))
    mixed = nn(normed_all, qkv_x) + jnp.concatenate([bias_q, jnp.zeros((256,), f32), bias_v])
    mixed = mixed.astype(bf16).reshape(NX, TOK, 3, NZ, 128)
    keep = lax.dynamic_index_in_dim(mixed, zl, 3, keepdims=False)
    come = take_from(lax.dynamic_index_in_dim(mixed, 1 - zl, 3, keepdims=False), dz=1)
    heads = jnp.zeros((NX, NZ, TOK, 3, 128), bf16)
    heads = put(put(heads, keep[:, None], zl, 1), come[:, None], 1 - zl, 1).reshape(SEQ, 3, 128)
    queries, keys, values = heads[:, 0], heads[:, 1], heads[:, 2]

    table = np.zeros((8, 8, 128), np.float32)
    for s in range(8):
        for h in range(2):
            rest = SLOPES[2 * s + h]
            for n in range(3):
                part = np.float32(np.asarray(rest).astype(jnp.bfloat16))
                rest = np.float32(rest - part)
                table[s, :, 64 * (1 - h) + n] = part
                table[s, :, 64 * (1 - h) + 3 + n] = part
    slopes = lax.dynamic_index_in_dim(jnp.asarray(table), shard, 0, keepdims=False)

    ctx_f, ctx_low, queries_back = attn_fwd(queries, keys, values, seg_col, slopes)
    context = lax.all_to_all(ctx_low.reshape(8, TOK, 128), "shard", 0, 0)
    context = context.transpose(1, 0, 2).reshape(TOK, D)

    middle = rows_in + nn(context, full_out) + biases[3]
    second_f, second_pull = jax.vjp(layer_norm, middle, gains[1], biases[4])
    second = second_f.astype(bf16)

    second_all = jnp.concatenate(gather_x(second))
    grad_all = jnp.concatenate(grad_blocks)
    before = nn(second_all, up_x) + up_row
    after_f, gelu_pull = jax.vjp(lambda inner: jax.nn.gelu(inner, approximate=True), before)
    after = after_f.astype(bf16)
    grad_after = nt(grad_all, down_x)
    grad_before = gelu_pull(grad_after)[0].astype(bf16)
    back = nt(grad_before, up_x).astype(bf16).reshape(NX, TOK, D)
    grad_second = functools.reduce(jnp.add, [p.astype(f32) for p in spread_x([back[r] for r in range(NX)])])

    ahead = nn(after, down_x).astype(bf16).reshape(NX, TOK, D)
    down_parts = spread_x([ahead[r] for r in range(NX)])
    result = middle + functools.reduce(jnp.add, [p.astype(f32) for p in down_parts]) + biases[5]
    hidden_out = result.astype(bf16)

    grad_up = tn(second_all, grad_before).astype(bf16).reshape(NX, NZ, 128, D)
    grad_down = tn(after, grad_all).astype(bf16).reshape(NZ, NX, 128, D).transpose(1, 0, 2, 3)
    grad_bias_up = jnp.sum(grad_before.astype(f32), axis=0)

    upstream = out_grad.astype(f32)
    grad_bias_down = jnp.sum(upstream, axis=0)
    grad_mid_norm, grad_gain_two, grad_shift_two = second_pull(grad_second)
    grad_middle = upstream + grad_mid_norm
    grad_branch = grad_middle.astype(bf16)
    grad_bias_out = jnp.sum(grad_branch.astype(f32), axis=0)
    grad_context = nt(grad_branch, full_out).astype(bf16)
    grad_out = tn(context, grad_branch).astype(bf16).reshape(NX, NZ, 128, D)
    grad_ctx = lax.all_to_all(grad_context.reshape(TOK, 8, 128), "shard", 1, 0).reshape(SEQ, 128)

    dq, dk, dv = attn_bwd(queries_back, keys, values, grad_ctx, ctx_f, seg_col)
    dmix = jnp.stack([dq, dk, dv], axis=1).reshape(NX, NZ, TOK, 3, 128)
    keep = lax.dynamic_index_in_dim(dmix, zl, 1, keepdims=False)
    come = take_from(lax.dynamic_index_in_dim(dmix, 1 - zl, 1, keepdims=False), dz=1)
    grad_mixed = jnp.zeros((NX, TOK, 3, NZ, 128), bf16)
    grad_mixed = put(put(grad_mixed, keep[:, :, :, None], zl, 3), come[:, :, :, None], 1 - zl, 3)
    grad_mixed = grad_mixed.reshape(NX * TOK, 768)
    low = nt(grad_mixed, qkv_x).astype(bf16).reshape(NX, TOK, D)
    low_parts = spread_x([lax.dynamic_index_in_dim(low, (x + r) % NX, 0, keepdims=False) for r in range(NX)])
    grad_normed = functools.reduce(jnp.add, [p.astype(f32) for p in low_parts])
    grad_qkv = tn(normed_all, grad_mixed).astype(bf16).reshape(NX, NZ, 128, 768)
    sums = jnp.sum(grad_mixed.astype(f32), axis=0)
    grad_in_norm, grad_gain_one, grad_shift_one = first_pull(grad_normed)
    in_grad = grad_middle + grad_in_norm

    ffn = jnp.concatenate([reduce_core_y(grad_up, core, y), reduce_core_y(grad_down, core, y)])
    out_held = reduce_core_y(grad_out, core, y)
    out_parts = spread_x([lax.dynamic_index_in_dim(out_held, (x + r) % NX, 0) for r in range(NX)])
    wide_held = jnp.concatenate([ffn, add_low(*out_parts)])
    wide_sum = reduce_z(reduce_y(wide_held, y), zl)
    up_sum = to_owner_x(wide_sum[:4], x)
    wide_all = gather_y_core(jnp.concatenate([up_sum, wide_sum[4:]]), y, core)
    final_up = wide_all[:4].reshape(NX, 128, D).transpose(1, 0, 2).reshape(128, 4 * D).astype(f32)
    final_down = wide_all[4:8].reshape(512, D).astype(f32)
    final_out = wide_all[8].reshape(128, D).astype(f32)

    qkv_sum = reduce_z(reduce_y(reduce_core_y(grad_qkv, core, y), y), zl)
    qkv_all = gather_y_core(to_owner_x(qkv_sum, x), y, core)
    final_qkv = qkv_all.reshape(NX, 128, 3, 256).transpose(1, 2, 0, 3).reshape(128, 3 * D).astype(f32)

    wide_row = lambda part: lax.dynamic_update_slice(jnp.zeros((D,), f32), part, (x * 256,))
    rows = jnp.stack(
        [
            grad_gain_one,
            grad_gain_two,
            grad_shift_one,
            wide_row(sums[:256]),
            wide_row(sums[512:]),
            grad_bias_out,
            grad_shift_two,
            grad_bias_down,
        ]
    )
    up_wide = lax.dynamic_update_slice(jnp.zeros((4 * D,), f32), grad_bias_up, (x * D,))
    small = jnp.concatenate(
        [rows.reshape(8, 8, 128).transpose(1, 0, 2), up_wide.reshape(8, 4, 128), jnp.zeros((8, 4, 128), f32)], axis=1
    )
    small = jnp.sum(lax.all_to_all(small, "shard", 0, 0), axis=0)
    small = jnp.sum(lax.all_to_all(jnp.broadcast_to(small[None], (16, 16, 128)), "replica", 0, 0), axis=0)

    return (
        hidden_out,
        in_grad,
        final_qkv,
        final_out,
        final_up,
        final_down,
        small[0:2],
        small[2:8],
        small[8:12].reshape(512),
    )


def solution(mesh):
    return jax.shard_map(
        per_device,
        mesh=mesh,
        in_specs=(
            P(("replica", "shard"), None),
            P(("replica", "shard")),
            P(("replica", "shard"), None),
            P("shard", None),
            P("shard", None),
            P("shard", None),
            P("shard", None),
            P(None, "shard"),
            P(None, "shard"),
            P("shard"),
        ),
        out_specs=(
            P(("replica", "shard"), None),
            P(("replica", "shard"), None),
            P("shard", None),
            P("shard", None),
            P("shard", None),
            P("shard", None),
            P(None, "shard"),
            P(None, "shard"),
            P("shard"),
        ),
        check_vma=False,
    )
```

```python
import functools

import jax
import jax.numpy as jnp
import numpy as np
from jax import lax
from jax.experimental import pallas as pl
from jax.experimental.pallas import tpu as pltpu
from jax.sharding import PartitionSpec as P

f32 = jnp.float32
bf16 = jnp.bfloat16

D = 1024
H = 16
HD = 64
TOK = 256
SEQ = 2048
NX, NZ, NY = 4, 2, 4
FWD_ROWS = 1024
BWD_ROWS = 512
FAR = -1e30

SLOPES = (2.0 ** (-8.0 * (np.arange(H) + 1) / H) / 128).astype(np.float32)


def nt(a, b):
    return lax.dot_general(a, b, (((1,), (1,)), ((), ())), preferred_element_type=f32)


def nn(a, b):
    return lax.dot_general(a, b, (((1,), (0,)), ((), ())), preferred_element_type=f32)


def tn(a, b):
    return lax.dot_general(a, b, (((0,), (0,)), ((), ())), preferred_element_type=f32)


def pieces(x):
    a = x.astype(bf16).astype(f32)
    r = x - a
    b = r.astype(bf16).astype(f32)
    return a, b, r - b


def lane_of(rows):
    return lax.broadcasted_iota(jnp.int32, (rows, 128), 1)


def key_features(seg_col, rows):
    feat = lane_of(rows) & 63
    pos = lax.broadcasted_iota(jnp.int32, (rows, 128), 0)
    coarse = (pos & -256).astype(f32)
    fine = (pos & 255).astype(f32)
    flag = (seg_col.astype(f32) == (feat - 9).astype(f32)).astype(f32)
    out = jnp.where(feat < 3, coarse, jnp.where(feat < 6, fine, jnp.where(feat < 9, 1.0, flag)))
    return jnp.where(feat < 14, out, 0.0).astype(bf16)


def join_rows(pos_ref, own_ref, come_ref, out_ref):
    zl = pos_ref[1]
    for n in range(NX):
        rows = pl.ds(n * TOK, TOK)
        for ref, side in ((own_ref, zl), (come_ref, 1 - zl)):
            out_ref[pl.ds(pl.multiple_of((2 * n + side) * TOK, TOK), TOK), :] = ref[rows, :]


def fwd_kernel(bq, pos_ref, own_ref, come_ref, seg_ref, segq_ref, slope_ref, c_ref, low_ref, qb_ref, h_s, k_s, vt_s, q_s):
    i = pl.program_id(0)

    @pl.when(i == 0)
    def _():
        join_rows(pos_ref, own_ref, come_ref, h_s)
        k_ref = h_s.at[:, 128:256]
        v_ref = h_s.at[:, 256:384]
        feats = key_features(seg_ref[...], SEQ)
        left = lane_of(SEQ) < 64
        k_s[0] = jnp.where(left, k_ref[...], feats)
        k_s[1] = jnp.where(left, feats, k_ref[...])
        vt = v_ref[...].T
        for h in range(2):
            vt_s[h, 0:64, :] = vt[64 * h : 64 * h + 64]
            vt_s[h, 64:80, :] = jnp.ones((16, SEQ), bf16)

    lane = lane_of(bq)
    feat = lane & 63
    left = lane < 64
    off = jnp.where(segq_ref[...].astype(f32) == (feat - 9).astype(f32), 0.0, FAR)
    base = jnp.where(feat < 9, slope_ref[0:1, :], jnp.where(feat < 14, off, 0.0))
    q = h_s[pl.ds(pl.multiple_of(i * bq, bq), bq), 0:128].astype(f32) * (HD**-0.5)
    q_s[0] = jnp.where(left, q, base).astype(bf16)
    q_s[1] = jnp.where(left, base, q).astype(bf16)

    def tile(j, carry, diag):
        out = []
        for h in range(2):
            top, acc = carry[h]
            s = nt(k_s[h, pl.ds(pl.multiple_of(j * bq, bq), bq), :], q_s[h])
            if diag:
                kk = lax.broadcasted_iota(jnp.int32, (bq, bq), 0)
                qq = lax.broadcasted_iota(jnp.int32, (bq, bq), 1)
                s = jnp.where(kk <= qq, s, FAR)
            new = jnp.maximum(top, jnp.max(s, axis=0, keepdims=True))
            p = jnp.exp(s - new).astype(bf16)
            o = nn(vt_s[h, :, pl.ds(pl.multiple_of(j * bq, bq), bq)], p)
            out.append((new, acc * jnp.exp(top - new) + o))
        return tuple(out)

    init = tuple((jnp.full((1, bq), FAR, f32), jnp.zeros((80, bq), f32)) for _ in range(2))
    carry = tile(i, init, True)
    carry = lax.fori_loop(0, i, lambda j, c: tile(j, c, False), carry)
    outs = []
    rows = lax.broadcasted_iota(jnp.int32, (128, bq), 0)
    spread = jnp.zeros((128, bq), f32)
    for h in range(2):
        top, acc = carry[h]
        total = acc[64:65]
        outs.append(acc[:64] / total)
        for n, part in enumerate(pieces(-(top + jnp.log(total)))):
            spread = jnp.where(rows == 64 * (1 - h) + 6 + n, part, spread)
    ctx = jnp.concatenate(outs, axis=0).T
    c_ref[...] = ctx
    low_ref[...] = ctx.astype(bf16)
    full = base + spread.T
    qb_ref[0] = jnp.where(left, q, full).astype(bf16)
    qb_ref[1] = jnp.where(left, full, q).astype(bf16)


def attn_fwd(pos, own, come, seg_col, slopes):
    bq = FWD_ROWS
    whole = pl.BlockSpec((SEQ // 2, 384), lambda i: (0, 0))
    block = pl.BlockSpec((bq, 128), lambda i: (i, 0))
    return pl.pallas_call(
        functools.partial(fwd_kernel, bq),
        grid=(SEQ // bq,),
        in_specs=[
            pl.BlockSpec(memory_space=pltpu.SMEM),
            whole,
            whole,
            pl.BlockSpec((SEQ, 1), lambda i: (0, 0)),
            pl.BlockSpec((bq, 1), lambda i: (i, 0)),
            pl.BlockSpec((8, 128), lambda i: (0, 0)),
        ],
        out_specs=[block, block, pl.BlockSpec((2, bq, 128), lambda i: (0, i, 0))],
        out_shape=[
            jax.ShapeDtypeStruct((SEQ, 128), f32),
            jax.ShapeDtypeStruct((SEQ, 128), bf16),
            jax.ShapeDtypeStruct((2, SEQ, 128), bf16),
        ],
        scratch_shapes=[
            pltpu.VMEM((SEQ, 384), bf16),
            pltpu.VMEM((2, SEQ, 128), bf16),
            pltpu.VMEM((2, 80, SEQ), bf16),
            pltpu.VMEM((2, bq, 128), bf16),
        ],
        compiler_params=pltpu.CompilerParams(vmem_limit_bytes=48 * 2**20),
        cost_estimate=pl.CostEstimate(flops=2 * 10**9, bytes_accessed=4 * 2**20, transcendentals=5 * 10**6),
        name="attn_fwd",
    )(pos, own, come, seg_col, seg_col, slopes)


def bwd_kernel(
    bq, pos_ref, q_ref, own_ref, come_ref, d_ref, c_ref, seg_ref, mine_ref, other_ref, h_s, out_ref, k_s, v_s, kt_s, d_s, dk_acc, dv_acc
):
    i = pl.program_id(0)
    n = pl.num_programs(0)

    @pl.when(i == 0)
    def _():
        join_rows(pos_ref, own_ref, come_ref, h_s)
        k_ref = h_s.at[:, 128:256]
        v_ref = h_s.at[:, 256:384]
        feats = key_features(seg_ref[...], SEQ)
        left = lane_of(SEQ) < 64
        k_s[0] = jnp.where(left, k_ref[...], feats)
        k_s[1] = jnp.where(left, feats, k_ref[...])
        v_s[0] = jnp.where(left, v_ref[...], feats)
        v_s[1] = jnp.where(left, feats, v_ref[...])
        kt_s[...] = k_ref[...].T

    lane = lane_of(bq)
    feat = lane & 63
    left = lane < 64
    grad = d_ref[...].astype(f32)
    prod = grad * c_ref[...]
    for h in range(2):
        mine = left if h == 0 else ~left
        a, b, c = pieces(-jnp.sum(jnp.where(mine, prod, 0.0), axis=1, keepdims=True))
        extra = jnp.where(feat == 6, a, jnp.where(feat == 7, b, jnp.where(feat == 8, c, 0.0)))
        d_s[h] = jnp.where(mine, grad, extra).astype(bf16)

    def tile(j, carry, diag):
        out = []
        rows = pl.ds(pl.multiple_of(j * bq, bq), bq)
        for h in range(2):
            s = nt(k_s[h, rows, :], q_ref[h])
            if diag:
                kk = lax.broadcasted_iota(jnp.int32, (bq, bq), 0)
                qq = lax.broadcasted_iota(jnp.int32, (bq, bq), 1)
                s = jnp.where(kk <= qq, s, FAR)
            p = jnp.exp(s)
            ds = (p * nt(v_s[h, rows, :], d_s[h])).astype(bf16)
            dv = nn(p.astype(bf16), d_s[h])
            dk = nn(ds, q_ref[h])
            if diag:
                dv_acc[h, rows, :] = dv
                dk_acc[h, rows, :] = dk
            else:
                dv_acc[h, rows, :] += dv
                dk_acc[h, rows, :] += dk
            out.append(carry[h] + nn(kt_s[64 * h : 64 * h + 64, rows], ds))
        return tuple(out)

    init = tuple(jnp.zeros((64, bq), f32) for _ in range(2))
    carry = tile(i, init, True)
    carry = lax.fori_loop(0, i, lambda j, c: tile(j, c, False), carry)
    dq = (jnp.concatenate(carry, axis=0) * (HD**-0.5)).T
    out_ref[pl.ds(pl.multiple_of(i * bq, bq), bq), 0:128] = dq.astype(bf16)

    @pl.when(i == n - 1)
    def _():
        side = lane_of(SEQ) < 64
        out_ref[:, 128:256] = jnp.where(side, dk_acc[0], dk_acc[1]).astype(bf16)
        out_ref[:, 256:384] = jnp.where(side, dv_acc[0], dv_acc[1]).astype(bf16)
        zl = pos_ref[1]
        for m in range(NX):
            rows = pl.ds(m * TOK, TOK)
            mine_ref[rows, :] = out_ref[pl.ds(pl.multiple_of((2 * m + zl) * TOK, TOK), TOK), :]
            other_ref[rows, :] = out_ref[pl.ds(pl.multiple_of((2 * m + 1 - zl) * TOK, TOK), TOK), :]


def attn_bwd(pos, qb, own, come, d, ctx, seg_col):
    bq = BWD_ROWS
    whole = pl.BlockSpec((SEQ // 2, 384), lambda i: (0, 0))
    block = pl.BlockSpec((bq, 128), lambda i: (i, 0))
    return pl.pallas_call(
        functools.partial(bwd_kernel, bq),
        grid=(SEQ // bq,),
        in_specs=[
            pl.BlockSpec(memory_space=pltpu.SMEM),
            pl.BlockSpec((2, bq, 128), lambda i: (0, i, 0)),
            whole,
            whole,
            block,
            block,
            pl.BlockSpec((SEQ, 1), lambda i: (0, 0)),
        ],
        out_specs=[whole, whole],
        out_shape=[jax.ShapeDtypeStruct((SEQ // 2, 384), bf16)] * 2,
        scratch_shapes=[
            pltpu.VMEM((SEQ, 384), bf16),
            pltpu.VMEM((SEQ, 384), bf16),
            pltpu.VMEM((2, SEQ, 128), bf16),
            pltpu.VMEM((2, SEQ, 128), bf16),
            pltpu.VMEM((128, SEQ), bf16),
            pltpu.VMEM((2, bq, 128), bf16),
            pltpu.VMEM((2, SEQ, 128), f32),
            pltpu.VMEM((2, SEQ, 128), f32),
        ],
        compiler_params=pltpu.CompilerParams(vmem_limit_bytes=48 * 2**20),
        cost_estimate=pl.CostEstimate(flops=5 * 10**9, bytes_accessed=6 * 2**20, transcendentals=5 * 10**6),
        name="attn_bwd",
    )(pos, qb, own, come, d, ctx, seg_col)


def call(kernel, outs, name, *args):
    smem = pl.BlockSpec(memory_space=pltpu.SMEM)
    vmem = pl.BlockSpec(memory_space=pltpu.VMEM)
    return pl.pallas_call(
        kernel,
        in_specs=[smem] + [vmem] * (len(args) - 1),
        out_specs=[vmem] * len(outs),
        out_shape=[jax.ShapeDtypeStruct(shape, dtype) for shape, dtype in outs],
        compiler_params=pltpu.CompilerParams(vmem_limit_bytes=48 * 2**20),
        name=name,
    )(*args)


def pick_kernel(pos_ref, w_ref, out_ref):
    x, zl = pos_ref[0], pos_ref[1]
    for r in range(NX):
        dest = lax.rem(x + r, NX)
        for half, pair in ((0, zl), (1, 1 - zl)):
            for c in range(3):
                start = pl.multiple_of(c * D + dest * 256 + pair * 128, 128)
                out_ref[r, :, pl.ds(half * 384 + c * 128, 128)] = w_ref[:, pl.ds(start, 128)]


def pick_up_kernel(pos_ref, w_ref, out_ref):
    for r in range(NX):
        start = pl.multiple_of(lax.rem(pos_ref[0] + r, NX) * D, D)
        out_ref[r] = w_ref[:, pl.ds(start, D)]


def first_kernel(
    pos_ref, own_ref, up_ref, down_ref, far_lo_ref, far_hi_ref, rows_ref, bias_ref, w0_ref, w1_ref, w2_ref, w3_ref,
    near_ref, cross_ref, other_ref, normed_ref, unit_ref, w_ref,
):
    x, zl, core = pos_ref[0], pos_ref[1], pos_ref[2]
    for r, ref in enumerate((w0_ref, w1_ref, w2_ref, w3_ref)):
        come = lax.rem(x - r + NX, NX)
        w_ref[pl.ds(pl.multiple_of((2 * come + zl) * 128, 128), 128), :] = ref[...]
        base = (2 * come + 1 - zl) * 128
        for part, side in ((near_ref, core), (cross_ref, 1 - core)):
            rows = pl.ds(pl.multiple_of(base + side * 64, 64), 64)
            w_ref[rows, :] = part[r]
    blocks = ((own_ref, 0, 0, 256), (up_ref, 1, 0, 256), (far_lo_ref, 2, 0, 128), (far_hi_ref, 2, 128, 128), (down_ref, 3, 0, 256))
    for ref, r, start, size in blocks:
        values = ref[...].astype(f32)
        center = values - jnp.mean(values, axis=-1, keepdims=True)
        spread = jnp.mean(center * center, axis=-1, keepdims=True)
        unit = center * lax.rsqrt(spread + 1e-05)
        normed = (unit * rows_ref[0:1, :] + rows_ref[1:2, :]).astype(bf16)
        rows = pl.ds(pl.multiple_of(lax.rem(x + r, NX) * TOK + start, 128), size)
        normed_ref[rows, :] = normed
        unit_ref[rows, :] = unit.astype(bf16)
        other_ref[rows, :] = (nn(normed, w_ref[:, 384:768]) + bias_ref[0:1, :]).astype(bf16)


def finish_ffn_kernel(pos_ref, mine_ref, come_ref, up_ref, down_ref):
    x, core, y = pos_ref[0], pos_ref[2], pos_ref[3]
    for ref, side in ((mine_ref, core), (come_ref, 1 - core)):
        for r in range(NY):
            row = pl.multiple_of(side * 64 + lax.rem(y + r, NY) * 16, 16)
            for n in range(NX):
                cols = pl.ds(pl.multiple_of(lax.rem(x - n + NX, NX) * D, D), D)
                up_ref[pl.ds(row, 16), cols] = ref[r, n].astype(f32)
                down_ref[pl.ds(pl.multiple_of(n * 128 + row, 16), 16), :] = ref[r, 4 + n].astype(f32)


def finish_last_kernel(pos_ref, mine_ref, come_ref, qkv_ref, out_ref):
    x, zl, core, y = pos_ref[0], pos_ref[1], pos_ref[2], pos_ref[3]
    for ref, side in ((mine_ref, core), (come_ref, 1 - core)):
        for r in range(NY):
            rows = pl.ds(pl.multiple_of(side * 64 + lax.rem(y + r, NY) * 16, 16), 16)
            for n in range(NX):
                block = ref[r, n].astype(f32)
                out_ref[rows, 256 * n : 256 * n + 256] = block[:, 768:1024]
                base = lax.rem(x - n + NX, NX) * 256
                for half, pair in ((0, zl), (1, 1 - zl)):
                    for c in range(3):
                        cols = pl.ds(pl.multiple_of(c * D + base + pair * 128, 128), 128)
                        qkv_ref[rows, cols] = block[:, half * 384 + c * 128 : half * 384 + c * 128 + 128]


def place(zh, y, c, x, zl):
    return ((zh * NY + y) * 2 + c) * 8 + x * NZ + zl


def take_from(array, dx=0, dz=0, dy=0, dc=0, dh=0):
    pairs = []
    for zh in range(2):
        for y in range(NY):
            for c in range(2):
                for x in range(NX):
                    for zl in range(NZ):
                        src = place((zh + dh) % 2, (y + dy) % NY, (c + dc) % 2, (x + dx) % NX, (zl + dz) % NZ)
                        pairs.append((src, place(zh, y, c, x, zl)))
    return lax.ppermute(array, ("replica", "shard"), pairs)


def piece(array, index, size, axis):
    return lax.dynamic_slice_in_dim(array, index * size, size, axis)


def put(target, value, index, axis):
    starts = [0] * target.ndim
    starts[axis] = index
    return lax.dynamic_update_slice(target, value.astype(target.dtype), starts)


def from_partner(array, axis, core):
    half = array.shape[axis] // 2
    mine = take_from(piece(array, core, half, axis), dz=1)
    other = take_from(mine, dc=1)
    out = jnp.zeros_like(array)
    return put(put(out, mine, core * half, axis), other, (1 - core) * half, axis)


def add_low(*parts):
    total = parts[0].astype(f32)
    for part in parts[1:]:
        total = total + part.astype(f32)
    return total.astype(bf16)


def spread_x(parts):
    return [parts[0]] + [take_from(parts[r], dx=-r) for r in range(1, NX)]


def ring_gather(block):
    half = block.shape[0] // 2
    up = take_from(block, dx=1)
    down = take_from(block, dx=-1)
    return [block, up, take_from(up[:half], dx=1), take_from(down[half:], dx=-1), down]


def ring_sum(parts):
    half = parts[0].shape[0] // 2
    low = take_from(parts[2][:half], dx=-1)
    high = take_from(parts[2][half:], dx=1)
    up = jnp.concatenate([add_low(parts[1][:half], low), parts[1][half:]])
    down = jnp.concatenate([parts[3][:half], add_low(parts[3][half:], high)])
    return parts[0].astype(f32) + take_from(up, dx=-1).astype(f32) + take_from(down, dx=1).astype(f32)


def after(values, *marks):
    return lax.optimization_barrier((values, marks))[0]


def normalize(values):
    center = values - jnp.mean(values, axis=-1, keepdims=True)
    spread = jnp.mean(center * center, axis=-1, keepdims=True)
    return center * lax.rsqrt(spread + 1e-05)


def layer_norm(values, gain, shift):
    return normalize(values) * gain + shift


def reduce_core(array, core):
    return add_low(piece(array, core, 64, 2), take_from(piece(array, 1 - core, 64, 2), dc=1))


def reduce_y(held, y):
    come = [take_from(piece(held, (y + r) % NY, 16, 2), dy=-r) for r in range(1, NY)]
    return add_low(piece(held, y, 16, 2), *come)


def reduce_z(held, zl, flip=None):
    own = jnp.squeeze(piece(held, zl, 1, 1), 1)
    other = jnp.squeeze(piece(held, 1 - zl, 1, 1), 1)
    if flip is not None:
        other = flip(other)
    near = own.astype(f32) + take_from(other, dz=1).astype(f32)
    far = take_from(own, dh=1).astype(f32) + take_from(other, dz=1, dh=1).astype(f32)
    return (near + far).astype(bf16)


def to_owner_x(part, x):
    return jnp.concatenate(spread_x([lax.dynamic_index_in_dim(part, (x + r) % NX, 0) for r in range(NX)]))


def gather_y(part):
    return jnp.stack([part] + [take_from(part, dy=r) for r in range(1, NY)])


def total(parts):
    return functools.reduce(jnp.add, [p.astype(f32) for p in parts])


def slope_table():
    table = np.zeros((8, 8, 128), np.float32)
    for s in range(8):
        for h in range(2):
            rest = SLOPES[2 * s + h]
            for n in range(3):
                part = np.float32(np.asarray(rest).astype(jnp.bfloat16))
                rest = np.float32(rest - part)
                table[s, :, 64 * (1 - h) + n] = part
                table[s, :, 64 * (1 - h) + 3 + n] = part
    return table


def per_device(hidden_in, segments, out_grad, w_qkv, w_out, w_up, w_down, norm_gains, bias_rows, up_bias):
    replica = lax.axis_index("replica")
    shard = lax.axis_index("shard")
    core = replica % 2
    y = (replica // 2) % NY
    x = shard // NZ
    zl = shard % NZ

    pack = jnp.concatenate(
        [
            norm_gains,
            bias_rows,
            up_bias.reshape(4, 128),
            segments.astype(bf16).reshape(2, 128),
            jnp.zeros((2, 128), bf16),
        ]
    )
    packs = lax.all_to_all(jnp.broadcast_to(pack[None], (8, 16, 128)), "shard", 0, 0)
    wide = packs.transpose(1, 0, 2).reshape(16, D).astype(f32)
    gains = wide[0:2]
    biases = wide[2:8]
    up_row = lax.dynamic_slice(packs[:, 8:12].reshape(NX, D), (x, 0), (1, D)).astype(f32)
    seg_col = packs[:, 12:14].reshape(SEQ).astype(f32).reshape(SEQ, 1)

    pos = jnp.stack([x, zl, core, y]).astype(jnp.int32)
    (send,) = call(pick_kernel, [((NX, 128, 768), bf16)], "pick_qkv", pos, w_qkv)
    come = spread_x([send[r] for r in range(NX)])
    half = jnp.stack([piece(part, core, 64, 0) for part in come])
    near = take_from(jnp.concatenate([half[..., 384:], half[..., :384]], axis=-1), dz=1)
    cross = take_from(near, dc=1)

    ring = ring_gather(after(hidden_in, send))

    def qkv_bias(pair):
        parts = [lax.dynamic_slice(biases[n], (x * 256 + pair * 128,), (128,)) for n in (1, 2)]
        return jnp.concatenate([parts[0], jnp.zeros((128,), f32), parts[1]])

    first_rows = jnp.stack([gains[0], biases[0]])
    mixed_other, normed_all, unit_all, qkv_x = call(
        first_kernel,
        [((NX * TOK, 384), bf16), ((NX * TOK, D), bf16), ((NX * TOK, D), bf16), ((D, 768), bf16)],
        "first_norm_qkv",
        pos,
        ring[0],
        ring[1],
        ring[4],
        ring[2],
        ring[3],
        first_rows,
        qkv_bias(1 - zl)[None],
        *come,
        near,
        cross,
    )
    mixed_come = take_from(mixed_other, dz=1)
    mixed_own = (nn(normed_all, qkv_x[:, :384]) + qkv_bias(zl)).astype(bf16)

    out_grad_b, w_up_b, w_out_b = after((out_grad, w_up, w_out), mixed_other)
    full_out = lax.all_gather(after(w_out, near), "shard", axis=0, tiled=True)
    (send,) = call(pick_up_kernel, [((NX, 128, D), bf16)], "pick_up", pos, w_up_b)
    come = spread_x([send[r] for r in range(NX)])
    grad_ring = ring_gather(out_grad_b)

    slopes = lax.dynamic_index_in_dim(jnp.asarray(slope_table()), shard, 0, keepdims=False)
    ctx_f, ctx_low, queries_back = attn_fwd(pos, mixed_own, mixed_come, seg_col, slopes)
    context = lax.all_to_all(ctx_low.reshape(8, TOK, 128), "shard", 0, 0)
    context = context.transpose(1, 0, 2).reshape(TOK, D)

    come = after(come, ctx_low)
    grad_ring = after(grad_ring, ctx_low)
    held = jnp.zeros((NX, 128, D), bf16)
    for r in range(NX):
        held = put(held, come[r], (x - r) % NX, 0) if come[r].ndim == 3 else put(held, come[r][None], (x - r) % NX, 0)
    w_down_b = after(w_down, mixed_come)
    other = from_partner(held, 1, core)
    up_x = jnp.zeros((NX, NZ, 128, D), bf16)
    up_x = put(put(up_x, held[:, None], zl, 1), other[:, None], 1 - zl, 1).reshape(D, D)
    down_other = after(from_partner(w_down_b, 0, core), ctx_low)
    down_x = jnp.zeros((NZ, 512, D), bf16)
    down_x = put(put(down_x, w_down[None], zl, 0), down_other[None], 1 - zl, 0).reshape(D, D)

    rows_in = hidden_in.astype(f32)
    middle = rows_in + nn(context, full_out) + biases[3]
    second_f, second_pull = jax.vjp(layer_norm, middle, gains[1], biases[4])
    second = second_f.astype(bf16)

    second_all = jnp.concatenate(ring_gather(second))
    grad_all = jnp.concatenate(grad_ring)
    before = nn(second_all, up_x) + up_row
    after_f, gelu_pull = jax.vjp(lambda inner: jax.nn.gelu(inner, approximate=True), before)
    act = after_f.astype(bf16)
    grad_act = nt(grad_all, down_x)
    grad_before = gelu_pull(grad_act)[0].astype(bf16)
    back = nt(grad_before, up_x).astype(bf16).reshape(NX, TOK, D)
    grad_second = ring_sum([back[r] for r in range(NX)])

    ahead = nn(act, down_x).astype(bf16)
    grad_up = tn(second_all, grad_before).astype(bf16).reshape(NX, NZ, 128, D)
    grad_down = tn(act, grad_all).astype(bf16).reshape(NZ, NX, 128, D)
    grad_bias_up = jnp.sum(grad_before.astype(f32), axis=0)
    up_held = reduce_core(grad_up, core)
    down_held = reduce_core(grad_down.transpose(1, 0, 2, 3), core)
    ffn_held = jnp.concatenate([up_held, down_held])

    upstream = out_grad.astype(f32)
    grad_bias_down = jnp.sum(upstream, axis=0)
    grad_mid_norm, grad_gain_two, grad_shift_two = second_pull(grad_second)
    grad_middle = upstream + grad_mid_norm
    grad_branch = grad_middle.astype(bf16)
    grad_bias_out = jnp.sum(grad_branch.astype(f32), axis=0)
    grad_context = nt(grad_branch, full_out).astype(bf16)
    grad_out = tn(context, grad_branch).astype(bf16).reshape(NX, NZ, 128, D)
    grad_ctx = lax.all_to_all(grad_context.reshape(TOK, 8, 128), "shard", 1, 0).reshape(SEQ, 128)
    ffn_y = reduce_y(ffn_held, y)

    ahead = after(ahead, grad_ctx).reshape(NX, TOK, D)
    down_parts = spread_x([ahead[r] for r in range(NX)])
    out_held = reduce_core(after(grad_out, grad_ctx), core)
    d_own, d_other = attn_bwd(pos, queries_back, mixed_own, mixed_come, grad_ctx, ctx_f, seg_col)
    d_own, d_other = after((d_own, d_other), down_parts, ffn_y, out_held)
    hidden_out = (middle + total(down_parts) + biases[5]).astype(bf16)

    d_come = take_from(d_other, dz=1)
    out_held = after(out_held, d_other)
    out_parts = spread_x([lax.dynamic_index_in_dim(out_held, (x + r) % NX, 0, keepdims=False) for r in range(NX)])
    out_sum = add_low(*out_parts)
    grad_own = tn(normed_all, d_own).astype(bf16)
    low_own = nt(d_own, qkv_x[:, :384])
    d_come = after(d_come, out_sum)

    grad_qkv = jnp.concatenate([grad_own, tn(normed_all, d_come).astype(bf16)], axis=1)
    qkv_held = reduce_core(grad_qkv.reshape(NX, NZ, 128, 768), core)
    low_f = low_own + nt(d_come, qkv_x[:, 384:])
    grad_gain_one = jnp.sum(low_f * unit_all.astype(f32), axis=0)
    grad_shift_one = jnp.sum(low_f, axis=0)
    low = low_f.astype(bf16).reshape(NX, TOK, D)
    grad_normed = ring_sum([lax.dynamic_index_in_dim(low, (x + r) % NX, 0, keepdims=False) for r in range(NX)])
    _, first_pull = jax.vjp(lambda rows: layer_norm(rows, gains[0], biases[0]), rows_in)
    in_grad = grad_middle + first_pull(grad_normed)[0]

    ffn_z = reduce_z(after(ffn_y, d_come), zl)
    ffn_part = gather_y(jnp.concatenate([to_owner_x(ffn_z[:4], x), ffn_z[4:]]))
    final_up, final_down = call(
        finish_ffn_kernel,
        [((128, 4 * D), f32), ((512, D), f32)],
        "finish_ffn",
        pos,
        ffn_part,
        take_from(ffn_part, dc=1),
    )

    out_side = out_sum.reshape(NZ, 64, 4, 256).transpose(2, 0, 1, 3)
    last_y = reduce_y(jnp.concatenate([qkv_held, out_side], axis=-1), y)
    turn = lambda part: jnp.concatenate([part[..., 384:768], part[..., :384], part[..., 768:]], axis=-1)
    last_z = reduce_z(last_y, zl, turn)
    last_part = gather_y(jnp.concatenate([to_owner_x(last_z[..., :768], x), last_z[..., 768:]], axis=-1))
    final_qkv, final_out = call(
        finish_last_kernel,
        [((128, 3 * D), f32), ((128, D), f32)],
        "finish_qkv",
        pos,
        last_part,
        take_from(last_part, dc=1),
    )

    sums_own = jnp.sum(d_own.astype(f32), axis=0)
    sums_come = jnp.sum(d_come.astype(f32), axis=0)

    def wide_row(n):
        row = jnp.zeros((D,), f32)
        row = lax.dynamic_update_slice(row, sums_own[128 * n : 128 * n + 128], (x * 256 + zl * 128,))
        return lax.dynamic_update_slice(row, sums_come[128 * n : 128 * n + 128], (x * 256 + (1 - zl) * 128,))

    rows = jnp.stack(
        [
            grad_gain_one,
            grad_gain_two,
            grad_shift_one,
            wide_row(0),
            wide_row(2),
            grad_bias_out,
            grad_shift_two,
            grad_bias_down,
        ]
    )
    up_wide = lax.dynamic_update_slice(jnp.zeros((4 * D,), f32), grad_bias_up, (x * D,))
    small = jnp.concatenate(
        [rows.reshape(8, 8, 128).transpose(1, 0, 2), up_wide.reshape(8, 4, 128), jnp.zeros((8, 4, 128), f32)], axis=1
    )
    small = jnp.sum(lax.all_to_all(small, "shard", 0, 0), axis=0)
    small = jnp.sum(lax.all_to_all(jnp.broadcast_to(small[None], (16, 16, 128)), "replica", 0, 0), axis=0)

    return (
        hidden_out,
        in_grad,
        final_qkv,
        final_out,
        final_up,
        final_down,
        small[0:2],
        small[2:8],
        small[8:12].reshape(512),
    )


def solution(mesh):
    return jax.shard_map(
        per_device,
        mesh=mesh,
        in_specs=(
            P(("replica", "shard"), None),
            P(("replica", "shard")),
            P(("replica", "shard"), None),
            P("shard", None),
            P("shard", None),
            P("shard", None),
            P("shard", None),
            P(None, "shard"),
            P(None, "shard"),
            P("shard"),
        ),
        out_specs=(
            P(("replica", "shard"), None),
            P(("replica", "shard"), None),
            P("shard", None),
            P("shard", None),
            P("shard", None),
            P("shard", None),
            P(None, "shard"),
            P(None, "shard"),
            P("shard"),
        ),
        check_vma=False,
    )
```

```python
import functools

import jax
import jax.numpy as jnp
import numpy as np
from jax import lax
from jax.experimental import pallas as pl
from jax.experimental.pallas import tpu as pltpu
from jax.sharding import PartitionSpec as P

f32 = jnp.float32
bf16 = jnp.bfloat16

D = 1024
H = 16
HD = 64
TOK = 256
SEQ = 2048
NX, NZ, NY = 4, 2, 4
FWD_ROWS = 1024
BWD_ROWS = 512
FAR = -1e30
VMEM_BYTES = 60 * 2**20

SLOPES = (2.0 ** (-8.0 * (np.arange(H) + 1) / H) / 128).astype(np.float32)


def nt(a, b):
    return lax.dot_general(a, b, (((1,), (1,)), ((), ())), preferred_element_type=f32)


def nn(a, b):
    return lax.dot_general(a, b, (((1,), (0,)), ((), ())), preferred_element_type=f32)


def tn(a, b):
    return lax.dot_general(a, b, (((0,), (0,)), ((), ())), preferred_element_type=f32)


def pieces(x):
    a = x.astype(bf16).astype(f32)
    r = x - a
    b = r.astype(bf16).astype(f32)
    return a, b, r - b


def lane_of(rows):
    return lax.broadcasted_iota(jnp.int32, (rows, 128), 1)


def key_features(seg_col, rows):
    feat = lane_of(rows) & 63
    pos = lax.broadcasted_iota(jnp.int32, (rows, 128), 0)
    coarse = (pos & -256).astype(f32)
    fine = (pos & 255).astype(f32)
    flag = (seg_col.astype(f32) == (feat - 9).astype(f32)).astype(f32)
    out = jnp.where(feat < 3, coarse, jnp.where(feat < 6, fine, jnp.where(feat < 9, 1.0, flag)))
    return jnp.where(feat < 14, out, 0.0).astype(bf16)


def join_rows(pos_ref, own_ref, come_ref, out_ref):
    zl = pos_ref[1]
    for n in range(NX):
        rows = pl.ds(n * TOK, TOK)
        for ref, side in ((own_ref, zl), (come_ref, 1 - zl)):
            out_ref[pl.ds(pl.multiple_of((2 * n + side) * TOK, TOK), TOK), :] = ref[rows, :]


def fwd_kernel(bq, pos_ref, own_ref, come_ref, seg_ref, segq_ref, slope_ref, c_ref, low_ref, qb_ref, h_s, k_s, vt_s, q_s):
    i = pl.program_id(0)

    @pl.when(i == 0)
    def _():
        join_rows(pos_ref, own_ref, come_ref, h_s)
        k_ref = h_s.at[:, 128:256]
        v_ref = h_s.at[:, 256:384]
        feats = key_features(seg_ref[...], SEQ)
        left = lane_of(SEQ) < 64
        k_s[0] = jnp.where(left, k_ref[...], feats)
        k_s[1] = jnp.where(left, feats, k_ref[...])
        vt = v_ref[...].T
        for h in range(2):
            vt_s[h, 0:64, :] = vt[64 * h : 64 * h + 64]
            vt_s[h, 64:80, :] = jnp.ones((16, SEQ), bf16)

    lane = lane_of(bq)
    feat = lane & 63
    left = lane < 64
    off = jnp.where(segq_ref[...].astype(f32) == (feat - 9).astype(f32), 0.0, FAR)
    base = jnp.where(feat < 9, slope_ref[0:1, :], jnp.where(feat < 14, off, 0.0))
    q = h_s[pl.ds(pl.multiple_of(i * bq, bq), bq), 0:128].astype(f32) * (HD**-0.5)
    q_s[0] = jnp.where(left, q, base).astype(bf16)
    q_s[1] = jnp.where(left, base, q).astype(bf16)

    def tile(j, carry, diag):
        out = []
        for h in range(2):
            top, acc = carry[h]
            s = nt(k_s[h, pl.ds(pl.multiple_of(j * bq, bq), bq), :], q_s[h])
            if diag:
                kk = lax.broadcasted_iota(jnp.int32, (bq, bq), 0)
                qq = lax.broadcasted_iota(jnp.int32, (bq, bq), 1)
                s = jnp.where(kk <= qq, s, FAR)
            new = jnp.maximum(top, jnp.max(s, axis=0, keepdims=True))
            p = jnp.exp(s - new).astype(bf16)
            o = nn(vt_s[h, :, pl.ds(pl.multiple_of(j * bq, bq), bq)], p)
            out.append((new, acc * jnp.exp(top - new) + o))
        return tuple(out)

    init = tuple((jnp.full((1, bq), FAR, f32), jnp.zeros((80, bq), f32)) for _ in range(2))
    carry = tile(i, init, True)
    carry = lax.fori_loop(0, i, lambda j, c: tile(j, c, False), carry)
    outs = []
    rows = lax.broadcasted_iota(jnp.int32, (128, bq), 0)
    spread = jnp.zeros((128, bq), f32)
    for h in range(2):
        top, acc = carry[h]
        total = acc[64:65]
        outs.append(acc[:64] / total)
        for n, part in enumerate(pieces(-(top + jnp.log(total)))):
            spread = jnp.where(rows == 64 * (1 - h) + 6 + n, part, spread)
    ctx = jnp.concatenate(outs, axis=0).T
    c_ref[...] = ctx
    low_ref[...] = ctx.astype(bf16)
    full = base + spread.T
    qb_ref[0] = jnp.where(left, q, full).astype(bf16)
    qb_ref[1] = jnp.where(left, full, q).astype(bf16)


def attn_fwd(pos, own, come, seg_col, slopes):
    bq = FWD_ROWS
    whole = pl.BlockSpec((SEQ // 2, 384), lambda i: (0, 0))
    block = pl.BlockSpec((bq, 128), lambda i: (i, 0))
    return pl.pallas_call(
        functools.partial(fwd_kernel, bq),
        grid=(SEQ // bq,),
        in_specs=[
            pl.BlockSpec(memory_space=pltpu.SMEM),
            whole,
            whole,
            pl.BlockSpec((SEQ, 1), lambda i: (0, 0)),
            pl.BlockSpec((bq, 1), lambda i: (i, 0)),
            pl.BlockSpec((8, 128), lambda i: (0, 0)),
        ],
        out_specs=[block, block, pl.BlockSpec((2, bq, 128), lambda i: (0, i, 0))],
        out_shape=[
            jax.ShapeDtypeStruct((SEQ, 128), f32),
            jax.ShapeDtypeStruct((SEQ, 128), bf16),
            jax.ShapeDtypeStruct((2, SEQ, 128), bf16),
        ],
        scratch_shapes=[
            pltpu.VMEM((SEQ, 384), bf16),
            pltpu.VMEM((2, SEQ, 128), bf16),
            pltpu.VMEM((2, 80, SEQ), bf16),
            pltpu.VMEM((2, bq, 128), bf16),
        ],
        compiler_params=pltpu.CompilerParams(vmem_limit_bytes=VMEM_BYTES),
        cost_estimate=pl.CostEstimate(flops=2 * 10**9, bytes_accessed=4 * 2**20, transcendentals=5 * 10**6),
        name="attn_fwd",
    )(pos, own, come, seg_col, seg_col, slopes)


def bwd_kernel(
    bq, pos_ref, q_ref, own_ref, come_ref, d_ref, c_ref, seg_ref, mine_ref, other_ref, h_s, out_ref, k_s, v_s, kt_s, d_s, dk_acc, dv_acc
):
    i = pl.program_id(0)
    n = pl.num_programs(0)

    @pl.when(i == 0)
    def _():
        join_rows(pos_ref, own_ref, come_ref, h_s)
        k_ref = h_s.at[:, 128:256]
        v_ref = h_s.at[:, 256:384]
        feats = key_features(seg_ref[...], SEQ)
        left = lane_of(SEQ) < 64
        k_s[0] = jnp.where(left, k_ref[...], feats)
        k_s[1] = jnp.where(left, feats, k_ref[...])
        v_s[0] = jnp.where(left, v_ref[...], feats)
        v_s[1] = jnp.where(left, feats, v_ref[...])
        kt_s[...] = k_ref[...].T

    lane = lane_of(bq)
    feat = lane & 63
    left = lane < 64
    grad = d_ref[...].astype(f32)
    prod = grad * c_ref[...]
    for h in range(2):
        mine = left if h == 0 else ~left
        a, b, c = pieces(-jnp.sum(jnp.where(mine, prod, 0.0), axis=1, keepdims=True))
        extra = jnp.where(feat == 6, a, jnp.where(feat == 7, b, jnp.where(feat == 8, c, 0.0)))
        d_s[h] = jnp.where(mine, grad, extra).astype(bf16)

    def tile(j, carry, diag):
        out = []
        rows = pl.ds(pl.multiple_of(j * bq, bq), bq)
        for h in range(2):
            s = nt(k_s[h, rows, :], q_ref[h])
            if diag:
                kk = lax.broadcasted_iota(jnp.int32, (bq, bq), 0)
                qq = lax.broadcasted_iota(jnp.int32, (bq, bq), 1)
                s = jnp.where(kk <= qq, s, FAR)
            p = jnp.exp(s)
            ds = (p * nt(v_s[h, rows, :], d_s[h])).astype(bf16)
            dv = nn(p.astype(bf16), d_s[h])
            dk = nn(ds, q_ref[h])
            if diag:
                dv_acc[h, rows, :] = dv
                dk_acc[h, rows, :] = dk
            else:
                dv_acc[h, rows, :] += dv
                dk_acc[h, rows, :] += dk
            out.append(carry[h] + nn(kt_s[64 * h : 64 * h + 64, rows], ds))
        return tuple(out)

    init = tuple(jnp.zeros((64, bq), f32) for _ in range(2))
    carry = tile(i, init, True)
    carry = lax.fori_loop(0, i, lambda j, c: tile(j, c, False), carry)
    dq = (jnp.concatenate(carry, axis=0) * (HD**-0.5)).T
    out_ref[pl.ds(pl.multiple_of(i * bq, bq), bq), 0:128] = dq.astype(bf16)

    @pl.when(i == n - 1)
    def _():
        side = lane_of(SEQ) < 64
        out_ref[:, 128:256] = jnp.where(side, dk_acc[0], dk_acc[1]).astype(bf16)
        out_ref[:, 256:384] = jnp.where(side, dv_acc[0], dv_acc[1]).astype(bf16)
        zl = pos_ref[1]
        for m in range(NX):
            rows = pl.ds(m * TOK, TOK)
            mine_ref[rows, :] = out_ref[pl.ds(pl.multiple_of((2 * m + zl) * TOK, TOK), TOK), :]
            other_ref[rows, :] = out_ref[pl.ds(pl.multiple_of((2 * m + 1 - zl) * TOK, TOK), TOK), :]


def attn_bwd(pos, qb, own, come, d, ctx, seg_col):
    bq = BWD_ROWS
    whole = pl.BlockSpec((SEQ // 2, 384), lambda i: (0, 0))
    block = pl.BlockSpec((bq, 128), lambda i: (i, 0))
    return pl.pallas_call(
        functools.partial(bwd_kernel, bq),
        grid=(SEQ // bq,),
        in_specs=[
            pl.BlockSpec(memory_space=pltpu.SMEM),
            pl.BlockSpec((2, bq, 128), lambda i: (0, i, 0)),
            whole,
            whole,
            block,
            block,
            pl.BlockSpec((SEQ, 1), lambda i: (0, 0)),
        ],
        out_specs=[whole, whole],
        out_shape=[jax.ShapeDtypeStruct((SEQ // 2, 384), bf16)] * 2,
        scratch_shapes=[
            pltpu.VMEM((SEQ, 384), bf16),
            pltpu.VMEM((SEQ, 384), bf16),
            pltpu.VMEM((2, SEQ, 128), bf16),
            pltpu.VMEM((2, SEQ, 128), bf16),
            pltpu.VMEM((128, SEQ), bf16),
            pltpu.VMEM((2, bq, 128), bf16),
            pltpu.VMEM((2, SEQ, 128), f32),
            pltpu.VMEM((2, SEQ, 128), f32),
        ],
        compiler_params=pltpu.CompilerParams(vmem_limit_bytes=VMEM_BYTES),
        cost_estimate=pl.CostEstimate(flops=5 * 10**9, bytes_accessed=6 * 2**20, transcendentals=5 * 10**6),
        name="attn_bwd",
    )(pos, qb, own, come, d, ctx, seg_col)


def call(kernel, outs, name, *args, scratch=()):
    smem = pl.BlockSpec(memory_space=pltpu.SMEM)
    vmem = pl.BlockSpec(memory_space=pltpu.VMEM)
    return pl.pallas_call(
        kernel,
        in_specs=[smem] + [vmem] * (len(args) - 1),
        out_specs=[vmem] * len(outs),
        out_shape=[jax.ShapeDtypeStruct(shape, dtype) for shape, dtype in outs],
        scratch_shapes=scratch,
        compiler_params=pltpu.CompilerParams(vmem_limit_bytes=VMEM_BYTES),
        name=name,
    )(*args)


def wide_kernel(pos_ref, *refs):
    *parts, wide_ref, up_ref, seg_ref = refs
    x, zl = pos_ref[0], pos_ref[1]
    for r in range(NX):
        for side, part in ((zl, parts[2 * r]), (1 - zl, parts[2 * r + 1])):
            owner = 2 * lax.rem(x + r, NX) + side
            cols = pl.ds(pl.multiple_of(owner * 128, 128), 128)
            wide_ref[:, cols] = part[0:16, :].astype(f32)
            seg_ref[pl.ds(pl.multiple_of(owner * 2, 2), 2), :] = part[12:14, :].astype(f32)
    for side, part in ((zl, parts[0]), (1 - zl, parts[1])):
        for n in range(4):
            cols = pl.ds(pl.multiple_of(side * 512 + n * 128, 128), 128)
            up_ref[0:1, cols] = part[8 + n : 9 + n, :].astype(f32)


def pick_kernel(pos_ref, w_ref, *out_refs):
    x, zl = pos_ref[0], pos_ref[1]
    for r in range(NX):
        dest = lax.rem(x + r, NX)
        for half, pair in ((0, zl), (1, 1 - zl)):
            for c in range(3):
                start = pl.multiple_of(c * D + dest * 256 + pair * 128, 128)
                out_refs[r][:, half * 384 + c * 128 : half * 384 + c * 128 + 128] = w_ref[:, pl.ds(start, 128)]


def pick_up_kernel(pos_ref, w_ref, near_ref, *out_refs):
    for r in range(NX):
        start = pl.multiple_of(lax.rem(pos_ref[0] + r, NX) * D, D)
        out_refs[r][0:128, :] = w_ref[:, pl.ds(start, D)]
        out_refs[r][128:192, :] = near_ref[:, pl.ds(start, D)]


def first_kernel(
    pos_ref, own_ref, up_ref, down_ref, far_ref, rows_ref, bias_ref, w0_ref, w1_ref, w2_ref, w3_ref,
    near_ref, cross_ref, other_ref, normed_ref, unit_ref, w_ref,
):
    x, zl, core = pos_ref[0], pos_ref[1], pos_ref[2]
    for r, ref in enumerate((w0_ref, w1_ref, w2_ref, w3_ref)):
        come = lax.rem(x - r + NX, NX)
        w_ref[pl.ds(pl.multiple_of((2 * come + zl) * 128, 128), 128), :] = ref[...]
        base = (2 * come + 1 - zl) * 128
        for part, side in ((near_ref, core), (cross_ref, 1 - core)):
            rows = pl.ds(pl.multiple_of(base + side * 64, 64), 64)
            w_ref[rows, :] = part[r]
    blocks = ((own_ref, 0, 0, 256), (up_ref, 1, 0, 256), (far_ref, 2, 0, 256), (down_ref, 3, 0, 256))
    for ref, r, start, size in blocks:
        values = ref[...].astype(f32)
        center = values - jnp.mean(values, axis=-1, keepdims=True)
        spread = jnp.mean(center * center, axis=-1, keepdims=True)
        unit = center * lax.rsqrt(spread + 1e-05)
        normed = (unit * rows_ref[0:1, :] + rows_ref[1:2, :]).astype(bf16)
        rows = pl.ds(pl.multiple_of(lax.rem(x + r, NX) * TOK + start, 128), size)
        normed_ref[rows, :] = normed
        unit_ref[rows, :] = unit.astype(bf16)
        other_ref[rows, :] = (nn(normed, w_ref[:, 384:768]) + bias_ref[0:1, :]).astype(bf16)


def ffn_kernel(
    pos_ref, own_ref, up_ref, down_ref, far_lo_ref, far_hi_ref, grad_ref, bias_ref, u0_ref, u1_ref, u2_ref, u3_ref,
    ucross_ref, d_ref, dnear_ref, dcross_ref,
    p0_ref, p1_ref, plo_ref, phi_ref, p3_ref, second_ref, act_ref, gb_ref, sum_ref, wd_ref, wu_s,
):
    x, zl, core = pos_ref[0], pos_ref[1], pos_ref[2]
    for r, ref in enumerate((u0_ref, u1_ref, u2_ref, u3_ref)):
        come = lax.rem(x - r + NX, NX)
        wu_s[pl.ds(pl.multiple_of((2 * come + zl) * 128, 128), 128), :] = ref[0:128, :]
        base = (2 * come + 1 - zl) * 128
        wu_s[pl.ds(pl.multiple_of(base + core * 64, 64), 64), :] = ref[128:192, :]
        wu_s[pl.ds(pl.multiple_of(base + (1 - core) * 64, 64), 64), :] = ucross_ref[r]
    wd_ref[pl.ds(pl.multiple_of(zl * 512, 512), 512), :] = d_ref[...]
    for part, side in ((dnear_ref, core), (dcross_ref, 1 - core)):
        wd_ref[pl.ds(pl.multiple_of((1 - zl) * 512 + side * 256, 256), 256), :] = part[...]
    blocks = (
        (own_ref, 0, 0, 256, p0_ref),
        (up_ref, 1, 0, 256, p1_ref),
        (down_ref, 3, 0, 256, p3_ref),
        (far_lo_ref, 2, 0, 128, plo_ref),
        (far_hi_ref, 2, 128, 128, phi_ref),
    )
    bias = jnp.zeros((1, D), f32)
    k0, k1 = np.float32(np.sqrt(2 / np.pi)), np.float32(0.044715)
    for ref, r, start, size, back_ref in blocks:
        rows = pl.ds(pl.multiple_of(lax.rem(x + r, NX) * TOK + start, 128), size)
        second = ref[...]
        second_ref[rows, :] = second
        z = nn(second, wu_s[...]) + bias_ref[0:1, :]
        sq = z * z
        t = jnp.tanh(k0 * z * (1.0 + k1 * sq))
        half = 0.5 * (1.0 + t)
        act_ref[rows, :] = (z * half).astype(bf16)
        slope = half + 0.5 * z * (1.0 - t * t) * (k0 * (1.0 + 3.0 * k1 * sq))
        gb = (slope * nt(grad_ref[rows, :], wd_ref[...])).astype(bf16)
        gb_ref[rows, :] = gb
        bias = bias + jnp.sum(gb.astype(f32), axis=0, keepdims=True)
        back_ref[...] = nt(gb, wu_s[...]).astype(bf16)
    sum_ref[0:1, :] = bias


def grad_qkv_kernel(pos_ref, normed_t_ref, own_ref, come_ref, keep_ref, send_ref, sum_ref):
    core = pos_ref[2]
    ones = jnp.ones((8, NX * TOK), bf16)
    for half, ref in ((0, own_ref), (1, come_ref)):
        cols = slice(half * 384, half * 384 + 384)
        sum_ref[:, cols] = nn(ones, ref[...])
        for n in range(8):
            part = nn(normed_t_ref[128 * n : 128 * n + 128, :], ref[...]).astype(bf16)
            first, second = part[:64], part[64:]
            keep_ref[n // 2, n % 2, :, cols] = jnp.where(core == 0, first, second)
            send_ref[n // 2, n % 2, :, cols] = jnp.where(core == 0, second, first)


def grad_normed_kernel(
    pos_ref, own_ref, come_ref, w_ref, unit_ref, p0_ref, p1_ref, far_lo_ref, far_hi_ref, p3_ref, sum_ref
):
    x = pos_ref[0]
    gain = jnp.zeros((1, D), f32)
    shift = jnp.zeros((1, D), f32)
    for r in range(NX):
        rows = pl.ds(pl.multiple_of(lax.rem(x + r, NX) * TOK, TOK), TOK)
        part = nt(own_ref[rows, :], w_ref[:, 0:384]) + nt(come_ref[rows, :], w_ref[:, 384:768])
        gain = gain + jnp.sum(part * unit_ref[rows, :].astype(f32), axis=0, keepdims=True)
        shift = shift + jnp.sum(part, axis=0, keepdims=True)
        low = part.astype(bf16)
        if r == 2:
            far_lo_ref[...] = low[:128]
            far_hi_ref[...] = low[128:]
        else:
            (p0_ref, p1_ref, None, p3_ref)[r][...] = low
    sum_ref[0:1, :] = gain
    sum_ref[1:2, :] = shift


def finish_ffn_kernel(pos_ref, all_ref, up_ref, down_ref):
    x = pos_ref[0]
    for n in range(NX):
        cols = pl.ds(pl.multiple_of(lax.rem(x - n + NX, NX) * D, D), D)
        for part in range(8):
            rows = slice(part * 16, part * 16 + 16)
            up_ref[rows, cols] = all_ref[part, n].astype(f32)
            down_ref[n * 128 + part * 16 : n * 128 + part * 16 + 16, :] = all_ref[part, 4 + n].astype(f32)


def finish_last_kernel(pos_ref, mine_ref, come_ref, qkv_ref, out_ref):
    x, zl, core, y = pos_ref[0], pos_ref[1], pos_ref[2], pos_ref[3]
    for ref, side in ((mine_ref, core), (come_ref, 1 - core)):
        for r in range(NY):
            rows = pl.ds(pl.multiple_of(side * 64 + lax.rem(y + r, NY) * 16, 16), 16)
            for n in range(NX):
                block = ref[r, n].astype(f32)
                out_ref[rows, 256 * n : 256 * n + 256] = block[:, 768:1024]
                base = lax.rem(x - n + NX, NX) * 256
                for half, pair in ((0, zl), (1, 1 - zl)):
                    for c in range(3):
                        cols = pl.ds(pl.multiple_of(c * D + base + pair * 128, 128), 128)
                        qkv_ref[rows, cols] = block[:, half * 384 + c * 128 : half * 384 + c * 128 + 128]


def place(zh, y, c, x, zl):
    return ((zh * NY + y) * 2 + c) * 8 + x * NZ + zl


def take_from(array, dx=0, dz=0, dy=0, dc=0, dh=0, flip_y=0):
    pairs = []
    for zh in range(2):
        for y in range(NY):
            for c in range(2):
                for x in range(NX):
                    for zl in range(NZ):
                        src = place((zh + dh) % 2, ((y ^ flip_y) + dy) % NY, (c + dc) % 2, (x + dx) % NX, (zl + dz) % NZ)
                        pairs.append((src, place(zh, y, c, x, zl)))
    return lax.ppermute(array, ("replica", "shard"), pairs)


def piece(array, index, size, axis):
    return lax.dynamic_slice_in_dim(array, index * size, size, axis)


def put(target, value, index, axis):
    starts = [0] * target.ndim
    starts[axis] = index
    return lax.dynamic_update_slice(target, value.astype(target.dtype), starts)


def from_partner(array, axis, core):
    half = array.shape[axis] // 2
    mine = take_from(piece(array, core, half, axis), dz=1)
    other = take_from(mine, dc=1)
    out = jnp.zeros_like(array)
    return put(put(out, mine, core * half, axis), other, (1 - core) * half, axis)


def add_low(*parts):
    total = parts[0].astype(f32)
    for part in parts[1:]:
        total = total + part.astype(f32)
    return total.astype(bf16)


Y_CORE = [[(zh * NY + y) * 2 + c for y in range(NY) for c in range(2)] for zh in range(2)]
X_RING = [[x * NZ + zl for x in range(NX)] for zl in range(NZ)]


def spread_x(parts):
    return [parts[0]] + [take_from(parts[r], dx=-r) for r in range(1, NX)]


def ring_gather(block):
    half = block.shape[0] // 2
    up = take_from(block, dx=1)
    down = take_from(block, dx=-1)
    return [block, up, take_from(up[:half], dx=1), take_from(down[half:], dx=-1), down]


def ring_sum(own, next_one, far_lo, far_hi, last):
    return ring_sum_end(own, next_one, *ring_sum_begin(far_lo, far_hi), last)


def ring_sum_begin(far_lo, far_hi):
    return take_from(far_lo, dx=-1), take_from(far_hi, dx=1)


def ring_sum_end(own, next_one, low, high, last):
    half = low.shape[0]
    up = jnp.concatenate([add_low(next_one[:half], low), next_one[half:]])
    down = jnp.concatenate([last[:half], add_low(last[half:], high)])
    return own.astype(f32) + take_from(up, dx=-1).astype(f32) + take_from(down, dx=1).astype(f32)


def after(values, *marks):
    return lax.optimization_barrier((values, marks))[0]


def normalize(values):
    center = values - jnp.mean(values, axis=-1, keepdims=True)
    spread = jnp.mean(center * center, axis=-1, keepdims=True)
    return center * lax.rsqrt(spread + 1e-05)


def layer_norm(values, gain, shift):
    return normalize(values) * gain + shift


def reduce_core(array, core):
    return add_low(piece(array, core, 64, 2), take_from(piece(array, 1 - core, 64, 2), dc=1))


def reduce_y(held, y):
    come = [take_from(piece(held, (y + r) % NY, 16, 2), dy=-r) for r in range(1, NY)]
    return add_low(piece(held, y, 16, 2), *come)


def reduce_z(held, zl, flip=None):
    own = jnp.squeeze(piece(held, zl, 1, 1), 1)
    other = jnp.squeeze(piece(held, 1 - zl, 1, 1), 1)
    if flip is not None:
        other = flip(other)
    near = own.astype(f32) + take_from(other, dz=1).astype(f32)
    far = take_from(own, dh=1).astype(f32) + take_from(other, dz=1, dh=1).astype(f32)
    return (near + far).astype(bf16)


def to_owner_x(part, x):
    return jnp.concatenate(spread_x([lax.dynamic_index_in_dim(part, (x + r) % NX, 0) for r in range(NX)]))


def gather_y(part):
    return jnp.stack([part] + [take_from(part, dy=r) for r in range(1, NY)])


def total(parts):
    return functools.reduce(jnp.add, [p.astype(f32) for p in parts])


def slope_table():
    table = np.zeros((8, 8, 128), np.float32)
    for s in range(8):
        for h in range(2):
            rest = SLOPES[2 * s + h]
            for n in range(3):
                part = np.float32(np.asarray(rest).astype(jnp.bfloat16))
                rest = np.float32(rest - part)
                table[s, :, 64 * (1 - h) + n] = part
                table[s, :, 64 * (1 - h) + 3 + n] = part
    return table


def per_device(hidden_in, segments, out_grad, w_qkv, w_out, w_up, w_down, norm_gains, bias_rows, up_bias):
    replica = lax.axis_index("replica")
    shard = lax.axis_index("shard")
    core = replica % 2
    y = (replica // 2) % NY
    x = shard // NZ
    zl = shard % NZ

    pack = jnp.concatenate(
        [
            norm_gains,
            bias_rows,
            up_bias.reshape(4, 128),
            segments.astype(bf16).reshape(2, 128),
            jnp.zeros((2, 128), bf16),
        ]
    )
    pos = jnp.stack([x, zl, core, y]).astype(jnp.int32)
    pack_near = take_from(pack, dz=1)
    pair = jnp.concatenate([pack, pack_near])
    pairs = [pair] + [take_from(pair, dx=r) for r in range(1, NX)]
    packs = [part[16 * n : 16 * n + 16] for part in pairs for n in range(2)]
    wide, up_row, seg_rows = call(
        wide_kernel, [((16, D), f32), ((8, D), f32), ((16, 128), f32)], "small_arrays", pos, *packs
    )
    gains = wide[0:2]
    biases = wide[2:8]
    seg_col = seg_rows.reshape(SEQ, 1)

    send = call(pick_kernel, [((128, 768), bf16)] * NX, "pick_qkv", pos, w_qkv)
    come = spread_x(send)
    hidden_b = after(hidden_in, send)
    ring_up = take_from(hidden_b, dx=1)
    ring_down = take_from(hidden_b, dx=-1)
    ring_far = take_from(hidden_b, dx=2)
    up_near = take_from(after(piece(w_up, core, 64, 0), send), dz=1)
    down_near = take_from(after(piece(w_down, core, 256, 0), send), dz=1)
    down_cross = take_from(down_near, dc=1)
    come_b = after(come, ring_up, ring_down, wide, up_near, down_near)
    half = jnp.stack([piece(part, core, 64, 0) for part in come_b])
    near = take_from(jnp.concatenate([half[..., 384:], half[..., :384]], axis=-1), dz=1)
    cross = take_from(near, dc=1)

    grad_all = lax.all_gather(after(out_grad, near), "shard", axis=0, axis_index_groups=X_RING, tiled=True)
    out_half = piece(after(w_out, send), core, 512, 1)
    out_near = take_from(out_half, dz=1)
    out_pair = jnp.where(zl == 0, jnp.concatenate([out_half, out_near]), jnp.concatenate([out_near, out_half]))
    out_mine = lax.all_gather(
        after(out_pair, come_b), "shard", axis=0, axis_index_groups=X_RING, tiled=True
    )


    def qkv_bias(pair):
        parts = [lax.dynamic_slice(biases[n], (x * 256 + pair * 128,), (128,)) for n in (1, 2)]
        return jnp.concatenate([parts[0], jnp.zeros((128,), f32), parts[1]])

    first_rows = jnp.stack([gains[0], biases[0]])
    mixed_other, normed_all, unit_all, qkv_x = call(
        first_kernel,
        [((NX * TOK, 384), bf16), ((NX * TOK, D), bf16), ((NX * TOK, D), bf16), ((D, 768), bf16)],
        "first_norm_qkv",
        pos,
        hidden_in,
        ring_up,
        ring_down,
        ring_far,
        first_rows,
        qkv_bias(1 - zl)[None],
        *come,
        near,
        cross,
    )
    mixed_come = take_from(mixed_other, dz=1)
    mixed_own = (nn(normed_all, qkv_x[:, :384]) + qkv_bias(zl)).astype(bf16)

    send = call(pick_up_kernel, [((192, D), bf16)] * NX, "pick_up", after(pos, mixed_other), w_up, up_near)
    come = spread_x(send)
    out_cross = take_from(after(out_mine, mixed_come), dc=1)
    normed_t = after(normed_all, mixed_other).T
    mixed_come = after(mixed_come, normed_t, come)

    slopes = lax.dynamic_index_in_dim(jnp.asarray(slope_table()), shard, 0, keepdims=False)
    ctx_f, ctx_low, queries_back = attn_fwd(pos, mixed_own, mixed_come, seg_col, slopes)
    context = lax.all_to_all(ctx_low.reshape(8, TOK, 128), "shard", 0, 0)
    context = context.transpose(1, 0, 2).reshape(TOK, D)

    out_mine, out_cross = after((out_mine, out_cross), ctx_low)
    out_left = jnp.where(core == 0, out_mine, out_cross)
    out_right = jnp.where(core == 0, out_cross, out_mine)

    rows_in = hidden_in.astype(f32)
    middle = rows_in + jnp.concatenate([nn(context, out_left), nn(context, out_right)], axis=1) + biases[3]
    second_f, second_pull = jax.vjp(layer_norm, middle, gains[1], biases[4])
    second = second_f.astype(bf16)

    up_cross = take_from(jnp.stack([part[128:192] for part in after(come, ctx_low)]), dc=1)
    ring = ring_gather(second)
    full = ((NX * TOK, D), bf16)
    *back, second_all, act, grad_before, grad_bias_up, down_x = call(
        ffn_kernel,
        [((TOK, D), bf16), ((TOK, D), bf16), ((128, D), bf16), ((128, D), bf16), ((TOK, D), bf16)]
        + [full, full, full, ((8, D), f32), full],
        "feed_forward",
        pos,
        ring[0],
        ring[1],
        ring[4],
        ring[2],
        ring[3],
        grad_all,
        up_row,
        *come,
        up_cross,
        w_down,
        down_near,
        down_cross,
        scratch=[pltpu.VMEM((D, D), bf16)],
    )
    grad_bias_up = grad_bias_up[0]
    low, high = ring_sum_begin(back[2], back[3])
    grad_second = ring_sum_end(back[0], back[1], low, high, back[4])

    second_all, act = after((second_all, act), low, high)
    grad_up = tn(second_all, grad_before).astype(bf16).reshape(NX, NZ, 128, D)
    grad_down = tn(act, grad_all).astype(bf16).reshape(NZ, NX, 128, D)
    ffn_parts = jnp.concatenate([grad_up, grad_down.transpose(1, 0, 2, 3)]).reshape(8, NZ, 8, 16, D)
    ffn_y = lax.psum_scatter(
        ffn_parts.transpose(2, 0, 1, 3, 4).reshape(-1, D),
        "replica",
        scatter_dimension=0,
        axis_index_groups=Y_CORE,
        tiled=True,
    ).reshape(8, NZ, 16, D)

    upstream = out_grad.astype(f32)
    grad_bias_down = jnp.sum(upstream, axis=0)
    grad_mid_norm, grad_gain_two, grad_shift_two = second_pull(grad_second)
    grad_middle = upstream + grad_mid_norm
    grad_branch = grad_middle.astype(bf16)
    grad_bias_out = jnp.sum(grad_branch.astype(f32), axis=0)
    grad_context = (nt(grad_branch[:, :512], out_left) + nt(grad_branch[:, 512:], out_right)).astype(bf16)
    grad_ctx = lax.all_to_all(grad_context.reshape(TOK, 8, 128), "shard", 1, 0).reshape(SEQ, 128)

    ahead = nn(act, after(down_x, grad_second)).astype(bf16)
    down_sum = lax.psum_scatter(
        after(ahead, grad_ctx), "shard", scatter_dimension=0, axis_index_groups=X_RING, tiled=True
    )
    grad_out = tn(context, grad_branch).astype(bf16).reshape(NX, NZ, 128, D)
    out_held = reduce_core(grad_out, core)
    d_own, d_other = attn_bwd(pos, queries_back, mixed_own, mixed_come, grad_ctx, ctx_f, seg_col)
    d_own, d_other = after((d_own, d_other), out_held)

    d_come = take_from(d_other, dz=1)
    out_held = after(out_held, d_other)
    out_parts = spread_x([lax.dynamic_index_in_dim(out_held, (x + r) % NX, 0, keepdims=False) for r in range(NX)])
    out_sum = add_low(*out_parts)
    ffn_z = reduce_z(after(ffn_y, d_come), zl)

    qkv_keep, qkv_send, sums = call(
        grad_qkv_kernel,
        [((NX, NZ, 64, 768), bf16), ((NX, NZ, 64, 768), bf16), ((8, 768), f32)],
        "grad_qkv",
        pos,
        normed_t,
        d_own,
        d_come,
    )
    qkv_held = add_low(qkv_keep, take_from(qkv_send, dc=1))
    *low, first_sums = call(
        grad_normed_kernel,
        [((TOK, D), bf16), ((TOK, D), bf16), ((128, D), bf16), ((128, D), bf16), ((TOK, D), bf16), ((8, D), f32)],
        "grad_normed",
        after(pos, sums),
        d_own,
        d_come,
        qkv_x,
        unit_all,
    )
    grad_gain_one, grad_shift_one = first_sums[0], first_sums[1]
    sums_own, sums_come = sums[0, :384], sums[0, 384:]

    def wide_row(n):
        row = jnp.zeros((D,), f32)
        row = lax.dynamic_update_slice(row, sums_own[128 * n : 128 * n + 128], (x * 256 + zl * 128,))
        return lax.dynamic_update_slice(row, sums_come[128 * n : 128 * n + 128], (x * 256 + (1 - zl) * 128,))

    rows = jnp.stack(
        [
            grad_gain_one,
            grad_gain_two,
            grad_shift_one,
            wide_row(0),
            wide_row(2),
            grad_bias_out,
            grad_shift_two,
            grad_bias_down,
        ]
    )
    up_wide = lax.dynamic_update_slice(jnp.zeros((4 * D,), f32), grad_bias_up, (x * D,))
    small = jnp.concatenate(
        [rows.reshape(8, 8, 128).transpose(1, 0, 2), up_wide.reshape(8, 4, 128), jnp.zeros((8, 4, 128), f32)], axis=1
    )
    small = jnp.sum(lax.all_to_all(small, "shard", 0, 0), axis=0)

    low_come, high_come = ring_sum_begin(low[2], low[3])
    ffn_x = to_owner_x(ffn_z[:4], x)
    low_come, high_come = after((low_come, high_come), qkv_held, small, ffn_z)
    grad_normed = ring_sum_end(low[0], low[1], low_come, high_come, low[4])
    out_side = jnp.stack([out_sum[..., 256 * n : 256 * n + 256] for n in range(4)])
    last_y = reduce_y(jnp.concatenate([qkv_held, out_side], axis=-1), y)
    for step in ({"dc": 1}, {"flip_y": 1}, {"dy": 2}, {"dh": 1}):
        small = small + take_from(small, **step)
    grad_normed = after(grad_normed, last_y, ffn_x)
    _, first_pull = jax.vjp(lambda rows: layer_norm(rows, gains[0], biases[0]), rows_in)
    in_grad = grad_middle + first_pull(grad_normed)[0]
    hidden_out = (middle + after(down_sum, first_sums).astype(f32) + biases[5]).astype(bf16)

    ffn_part = jnp.concatenate([ffn_x, ffn_z[4:]])
    final_up, final_down = call(
        finish_ffn_kernel,
        [((128, 4 * D), f32), ((512, D), f32)],
        "finish_ffn",
        pos,
        lax.all_gather(ffn_part, "replica", axis=0, axis_index_groups=Y_CORE),
    )

    turn = lambda part: jnp.concatenate([part[..., 384:768], part[..., :384], part[..., 768:]], axis=-1)
    last_z = reduce_z(last_y, zl, turn)
    last_part = gather_y(jnp.concatenate([to_owner_x(last_z[..., :768], x), last_z[..., 768:]], axis=-1))
    final_qkv, final_out = call(
        finish_last_kernel,
        [((128, 3 * D), f32), ((128, D), f32)],
        "finish_qkv",
        pos,
        last_part,
        take_from(last_part, dc=1),
    )

    return (
        hidden_out,
        in_grad,
        final_qkv,
        final_out,
        final_up,
        final_down,
        small[0:2],
        small[2:8],
        small[8:12].reshape(512),
    )


def solution(mesh):
    return jax.shard_map(
        per_device,
        mesh=mesh,
        in_specs=(
            P(("replica", "shard"), None),
            P(("replica", "shard")),
            P(("replica", "shard"), None),
            P("shard", None),
            P("shard", None),
            P("shard", None),
            P("shard", None),
            P(None, "shard"),
            P(None, "shard"),
            P("shard"),
        ),
        out_specs=(
            P(("replica", "shard"), None),
            P(("replica", "shard"), None),
            P("shard", None),
            P("shard", None),
            P("shard", None),
            P("shard", None),
            P(None, "shard"),
            P(None, "shard"),
            P("shard"),
        ),
        check_vma=False,
    )
```

```python
import functools

import jax
import jax.numpy as jnp
import numpy as np
from jax import lax
from jax.experimental import pallas as pl
from jax.experimental.pallas import tpu as pltpu
from jax.sharding import PartitionSpec as P

f32 = jnp.float32
bf16 = jnp.bfloat16

D = 1024
H = 16
HD = 64
TOK = 256
SEQ = 2048
NX, NZ, NY = 4, 2, 4
FWD_ROWS = 1024
BWD_ROWS = 512
FAR = -1e30
VMEM_BYTES = 60 * 2**20

SLOPES = (2.0 ** (-8.0 * (np.arange(H) + 1) / H) / 128).astype(np.float32)


def nt(a, b):
    return lax.dot_general(a, b, (((1,), (1,)), ((), ())), preferred_element_type=f32)


def nn(a, b):
    return lax.dot_general(a, b, (((1,), (0,)), ((), ())), preferred_element_type=f32)


def tn(a, b):
    return lax.dot_general(a, b, (((0,), (0,)), ((), ())), preferred_element_type=f32)


def pieces(x):
    a = x.astype(bf16).astype(f32)
    r = x - a
    b = r.astype(bf16).astype(f32)
    return a, b, r - b


def lane_of(rows):
    return lax.broadcasted_iota(jnp.int32, (rows, 128), 1)


def key_features(seg_col, rows):
    feat = lane_of(rows) & 63
    pos = lax.broadcasted_iota(jnp.int32, (rows, 128), 0)
    coarse = (pos & -256).astype(f32)
    fine = (pos & 255).astype(f32)
    flag = (seg_col.astype(f32) == (feat - 9).astype(f32)).astype(f32)
    out = jnp.where(feat < 3, coarse, jnp.where(feat < 6, fine, jnp.where(feat < 9, 1.0, flag)))
    return jnp.where(feat < 14, out, 0.0).astype(bf16)


def join_rows(pos_ref, own_ref, come_ref, out_ref):
    zl = pos_ref[1]
    for n in range(NX):
        rows = pl.ds(n * TOK, TOK)
        for ref, side in ((own_ref, zl), (come_ref, 1 - zl)):
            out_ref[pl.ds(pl.multiple_of((2 * n + side) * TOK, TOK), TOK), :] = ref[rows, :]


def fwd_kernel(bq, pos_ref, own_ref, come_ref, seg_ref, segq_ref, slope_ref, c_ref, low_ref, qb_ref, h_s, k_s, vt_s, q_s):
    i = pl.program_id(0)

    @pl.when(i == 0)
    def _():
        join_rows(pos_ref, own_ref, come_ref, h_s)
        k_ref = h_s.at[:, 128:256]
        v_ref = h_s.at[:, 256:384]
        feats = key_features(seg_ref[...], SEQ)
        left = lane_of(SEQ) < 64
        k_s[0] = jnp.where(left, k_ref[...], feats)
        k_s[1] = jnp.where(left, feats, k_ref[...])
        vt = v_ref[...].T
        for h in range(2):
            vt_s[h, 0:64, :] = vt[64 * h : 64 * h + 64]
            vt_s[h, 64:80, :] = jnp.ones((16, SEQ), bf16)

    lane = lane_of(bq)
    feat = lane & 63
    left = lane < 64
    off = jnp.where(segq_ref[...].astype(f32) == (feat - 9).astype(f32), 0.0, FAR)
    base = jnp.where(feat < 9, slope_ref[0:1, :], jnp.where(feat < 14, off, 0.0))
    q = h_s[pl.ds(pl.multiple_of(i * bq, bq), bq), 0:128].astype(f32) * (HD**-0.5)
    q_s[0] = jnp.where(left, q, base).astype(bf16)
    q_s[1] = jnp.where(left, base, q).astype(bf16)

    def tile(j, carry, diag):
        out = []
        for h in range(2):
            top, acc = carry[h]
            s = nt(k_s[h, pl.ds(pl.multiple_of(j * bq, bq), bq), :], q_s[h])
            if diag:
                kk = lax.broadcasted_iota(jnp.int32, (bq, bq), 0)
                qq = lax.broadcasted_iota(jnp.int32, (bq, bq), 1)
                s = jnp.where(kk <= qq, s, FAR)
            new = jnp.maximum(top, jnp.max(s, axis=0, keepdims=True))
            p = jnp.exp(s - new).astype(bf16)
            o = nn(vt_s[h, :, pl.ds(pl.multiple_of(j * bq, bq), bq)], p)
            out.append((new, acc * jnp.exp(top - new) + o))
        return tuple(out)

    init = tuple((jnp.full((1, bq), FAR, f32), jnp.zeros((80, bq), f32)) for _ in range(2))
    carry = tile(i, init, True)
    carry = lax.fori_loop(0, i, lambda j, c: tile(j, c, False), carry)
    outs = []
    rows = lax.broadcasted_iota(jnp.int32, (128, bq), 0)
    spread = jnp.zeros((128, bq), f32)
    for h in range(2):
        top, acc = carry[h]
        total = acc[64:65]
        outs.append(acc[:64] / total)
        for n, part in enumerate(pieces(-(top + jnp.log(total)))):
            spread = jnp.where(rows == 64 * (1 - h) + 6 + n, part, spread)
    ctx = jnp.concatenate(outs, axis=0).T
    c_ref[...] = ctx
    low_ref[...] = ctx.astype(bf16)
    full = base + spread.T
    qb_ref[0] = jnp.where(left, q, full).astype(bf16)
    qb_ref[1] = jnp.where(left, full, q).astype(bf16)


def attn_fwd(pos, own, come, seg_col, slopes):
    bq = FWD_ROWS
    whole = pl.BlockSpec((SEQ // 2, 384), lambda i: (0, 0))
    block = pl.BlockSpec((bq, 128), lambda i: (i, 0))
    return pl.pallas_call(
        functools.partial(fwd_kernel, bq),
        grid=(SEQ // bq,),
        in_specs=[
            pl.BlockSpec(memory_space=pltpu.SMEM),
            whole,
            whole,
            pl.BlockSpec((SEQ, 1), lambda i: (0, 0)),
            pl.BlockSpec((bq, 1), lambda i: (i, 0)),
            pl.BlockSpec((8, 128), lambda i: (0, 0)),
        ],
        out_specs=[block, block, pl.BlockSpec((2, bq, 128), lambda i: (0, i, 0))],
        out_shape=[
            jax.ShapeDtypeStruct((SEQ, 128), f32),
            jax.ShapeDtypeStruct((SEQ, 128), bf16),
            jax.ShapeDtypeStruct((2, SEQ, 128), bf16),
        ],
        scratch_shapes=[
            pltpu.VMEM((SEQ, 384), bf16),
            pltpu.VMEM((2, SEQ, 128), bf16),
            pltpu.VMEM((2, 80, SEQ), bf16),
            pltpu.VMEM((2, bq, 128), bf16),
        ],
        compiler_params=pltpu.CompilerParams(vmem_limit_bytes=VMEM_BYTES),
        cost_estimate=pl.CostEstimate(flops=14 * 10**9, bytes_accessed=4 * 2**20, transcendentals=5 * 10**6),
        name="attn_fwd",
    )(pos, own, come, seg_col, seg_col, slopes)


def bwd_kernel(
    bq, pos_ref, q_ref, own_ref, come_ref, d_ref, c_ref, seg_ref, mine_ref, other_ref, h_s, out_ref, k_s, v_s, kt_s, d_s, dk_acc, dv_acc
):
    i = pl.program_id(0)
    n = pl.num_programs(0)

    @pl.when(i == 0)
    def _():
        join_rows(pos_ref, own_ref, come_ref, h_s)
        k_ref = h_s.at[:, 128:256]
        v_ref = h_s.at[:, 256:384]
        feats = key_features(seg_ref[...], SEQ)
        left = lane_of(SEQ) < 64
        k_s[0] = jnp.where(left, k_ref[...], feats)
        k_s[1] = jnp.where(left, feats, k_ref[...])
        v_s[0] = jnp.where(left, v_ref[...], feats)
        v_s[1] = jnp.where(left, feats, v_ref[...])
        kt_s[...] = k_ref[...].T

    lane = lane_of(bq)
    feat = lane & 63
    left = lane < 64
    grad = d_ref[...].astype(f32)
    prod = grad * c_ref[...]
    for h in range(2):
        mine = left if h == 0 else ~left
        a, b, c = pieces(-jnp.sum(jnp.where(mine, prod, 0.0), axis=1, keepdims=True))
        extra = jnp.where(feat == 6, a, jnp.where(feat == 7, b, jnp.where(feat == 8, c, 0.0)))
        d_s[h] = jnp.where(mine, grad, extra).astype(bf16)

    def tile(j, carry, diag):
        out = []
        rows = pl.ds(pl.multiple_of(j * bq, bq), bq)
        for h in range(2):
            s = nt(k_s[h, rows, :], q_ref[h])
            if diag:
                kk = lax.broadcasted_iota(jnp.int32, (bq, bq), 0)
                qq = lax.broadcasted_iota(jnp.int32, (bq, bq), 1)
                s = jnp.where(kk <= qq, s, FAR)
            p = jnp.exp(s)
            ds = (p * nt(v_s[h, rows, :], d_s[h])).astype(bf16)
            dv = nn(p.astype(bf16), d_s[h])
            dk = nn(ds, q_ref[h])
            if diag:
                dv_acc[h, rows, :] = dv
                dk_acc[h, rows, :] = dk
            else:
                dv_acc[h, rows, :] += dv
                dk_acc[h, rows, :] += dk
            out.append(carry[h] + nn(kt_s[64 * h : 64 * h + 64, rows], ds))
        return tuple(out)

    init = tuple(jnp.zeros((64, bq), f32) for _ in range(2))
    carry = tile(i, init, True)
    carry = lax.fori_loop(0, i, lambda j, c: tile(j, c, False), carry)
    dq = (jnp.concatenate(carry, axis=0) * (HD**-0.5)).T
    out_ref[pl.ds(pl.multiple_of(i * bq, bq), bq), 0:128] = dq.astype(bf16)

    @pl.when(i == n - 1)
    def _():
        side = lane_of(SEQ) < 64
        out_ref[:, 128:256] = jnp.where(side, dk_acc[0], dk_acc[1]).astype(bf16)
        out_ref[:, 256:384] = jnp.where(side, dv_acc[0], dv_acc[1]).astype(bf16)
        zl = pos_ref[1]
        for m in range(NX):
            rows = pl.ds(m * TOK, TOK)
            mine_ref[rows, :] = out_ref[pl.ds(pl.multiple_of((2 * m + zl) * TOK, TOK), TOK), :]
            other_ref[rows, :] = out_ref[pl.ds(pl.multiple_of((2 * m + 1 - zl) * TOK, TOK), TOK), :]


def attn_bwd(pos, qb, own, come, d, ctx, seg_col):
    bq = BWD_ROWS
    whole = pl.BlockSpec((SEQ // 2, 384), lambda i: (0, 0))
    block = pl.BlockSpec((bq, 128), lambda i: (i, 0))
    return pl.pallas_call(
        functools.partial(bwd_kernel, bq),
        grid=(SEQ // bq,),
        in_specs=[
            pl.BlockSpec(memory_space=pltpu.SMEM),
            pl.BlockSpec((2, bq, 128), lambda i: (0, i, 0)),
            whole,
            whole,
            block,
            block,
            pl.BlockSpec((SEQ, 1), lambda i: (0, 0)),
        ],
        out_specs=[whole, whole],
        out_shape=[jax.ShapeDtypeStruct((SEQ // 2, 384), bf16)] * 2,
        scratch_shapes=[
            pltpu.VMEM((SEQ, 384), bf16),
            pltpu.VMEM((SEQ, 384), bf16),
            pltpu.VMEM((2, SEQ, 128), bf16),
            pltpu.VMEM((2, SEQ, 128), bf16),
            pltpu.VMEM((128, SEQ), bf16),
            pltpu.VMEM((2, bq, 128), bf16),
            pltpu.VMEM((2, SEQ, 128), f32),
            pltpu.VMEM((2, SEQ, 128), f32),
        ],
        compiler_params=pltpu.CompilerParams(vmem_limit_bytes=VMEM_BYTES),
        cost_estimate=pl.CostEstimate(flops=23 * 10**9, bytes_accessed=6 * 2**20, transcendentals=5 * 10**6),
        name="attn_bwd",
    )(pos, qb, own, come, d, ctx, seg_col)


def call(kernel, outs, name, *args, scratch=(), flops=10**9):
    smem = pl.BlockSpec(memory_space=pltpu.SMEM)
    vmem = pl.BlockSpec(memory_space=pltpu.VMEM)
    return pl.pallas_call(
        kernel,
        in_specs=[smem] + [vmem] * (len(args) - 1),
        out_specs=[vmem] * len(outs),
        out_shape=[jax.ShapeDtypeStruct(shape, dtype) for shape, dtype in outs],
        scratch_shapes=scratch,
        cost_estimate=pl.CostEstimate(flops=flops, bytes_accessed=2**20, transcendentals=0),
        compiler_params=pltpu.CompilerParams(vmem_limit_bytes=VMEM_BYTES),
        name=name,
    )(*args)


def wide_kernel(pos_ref, *refs):
    *parts, wide_ref, up_ref, seg_ref = refs
    x, zl = pos_ref[0], pos_ref[1]
    for r in range(NX):
        for side, part in ((zl, parts[2 * r]), (1 - zl, parts[2 * r + 1])):
            owner = 2 * lax.rem(x + r, NX) + side
            cols = pl.ds(pl.multiple_of(owner * 128, 128), 128)
            wide_ref[:, cols] = part[0:16, :].astype(f32)
            seg_ref[pl.ds(pl.multiple_of(owner * 2, 2), 2), :] = part[12:14, :].astype(f32)
    for side, part in ((zl, parts[0]), (1 - zl, parts[1])):
        for n in range(4):
            cols = pl.ds(pl.multiple_of(side * 512 + n * 128, 128), 128)
            up_ref[0:1, cols] = part[8 + n : 9 + n, :].astype(f32)


def pick_kernel(pos_ref, w_ref, *out_refs):
    x, zl = pos_ref[0], pos_ref[1]
    for r in range(NX):
        dest = lax.rem(x + r, NX)
        for half, pair in ((0, zl), (1, 1 - zl)):
            for c in range(3):
                start = pl.multiple_of(c * D + dest * 256 + pair * 128, 128)
                out_refs[r][:, half * 384 + c * 128 : half * 384 + c * 128 + 128] = w_ref[:, pl.ds(start, 128)]


def pick_up_kernel(pos_ref, w_ref, near_ref, *out_refs):
    for r in range(NX):
        start = pl.multiple_of(lax.rem(pos_ref[0] + r, NX) * D, D)
        out_refs[r][0:128, :] = w_ref[:, pl.ds(start, D)]
        out_refs[r][128:192, :] = near_ref[:, pl.ds(start, D)]


def first_kernel(
    pos_ref, own_ref, up_ref, down_ref, far_lo_ref, far_hi_ref, rows_ref, bias_ref, w0_ref, w1_ref, w2_ref, w3_ref,
    near_ref, cross_ref, other_ref, normed_ref, unit_ref, w_ref,
):
    x, zl, core = pos_ref[0], pos_ref[1], pos_ref[2]
    for r, ref in enumerate((w0_ref, w1_ref, w2_ref, w3_ref)):
        come = lax.rem(x - r + NX, NX)
        w_ref[pl.ds(pl.multiple_of((2 * come + zl) * 128, 128), 128), :] = ref[...]
        base = (2 * come + 1 - zl) * 128
        for part, side in ((near_ref, core), (cross_ref, 1 - core)):
            rows = pl.ds(pl.multiple_of(base + side * 64, 64), 64)
            w_ref[rows, :] = part[r]
    blocks = ((own_ref, 0, 0, 256), (up_ref, 1, 0, 256), (far_lo_ref, 2, 0, 128), (far_hi_ref, 2, 128, 128), (down_ref, 3, 0, 256))
    for ref, r, start, size in blocks:
        values = ref[...].astype(f32)
        center = values - jnp.mean(values, axis=-1, keepdims=True)
        spread = jnp.mean(center * center, axis=-1, keepdims=True)
        unit = center * lax.rsqrt(spread + 1e-05)
        normed = (unit * rows_ref[0:1, :] + rows_ref[1:2, :]).astype(bf16)
        rows = pl.ds(pl.multiple_of(lax.rem(x + r, NX) * TOK + start, 128), size)
        normed_ref[rows, :] = normed
        unit_ref[rows, :] = unit.astype(bf16)
        other_ref[rows, :] = (nn(normed, w_ref[:, 384:768]) + bias_ref[0:1, :]).astype(bf16)


def ffn_kernel(
    pos_ref, own_ref, up_ref, down_ref, far_lo_ref, far_hi_ref, grad_ref, bias_ref, u0_ref, u1_ref, u2_ref, u3_ref,
    ucross_ref, d_ref, dnear_ref, dcross_ref,
    p0_ref, p1_ref, plo_ref, phi_ref, p3_ref, second_ref, act_ref, gb_ref, sum_ref, wd_ref, wu_s,
):
    x, zl, core = pos_ref[0], pos_ref[1], pos_ref[2]
    for r, ref in enumerate((u0_ref, u1_ref, u2_ref, u3_ref)):
        come = lax.rem(x - r + NX, NX)
        wu_s[pl.ds(pl.multiple_of((2 * come + zl) * 128, 128), 128), :] = ref[0:128, :]
        base = (2 * come + 1 - zl) * 128
        wu_s[pl.ds(pl.multiple_of(base + core * 64, 64), 64), :] = ref[128:192, :]
        wu_s[pl.ds(pl.multiple_of(base + (1 - core) * 64, 64), 64), :] = ucross_ref[r]
    wd_ref[pl.ds(pl.multiple_of(zl * 512, 512), 512), :] = d_ref[...]
    for part, side in ((dnear_ref, core), (dcross_ref, 1 - core)):
        wd_ref[pl.ds(pl.multiple_of((1 - zl) * 512 + side * 256, 256), 256), :] = part[...]
    blocks = (
        (own_ref, 0, 0, 256, p0_ref),
        (up_ref, 1, 0, 256, p1_ref),
        (down_ref, 3, 0, 256, p3_ref),
        (far_lo_ref, 2, 0, 128, plo_ref),
        (far_hi_ref, 2, 128, 128, phi_ref),
    )
    bias = jnp.zeros((1, D), f32)
    k0, k1 = np.float32(np.sqrt(2 / np.pi)), np.float32(0.044715)
    for ref, r, start, size, back_ref in blocks:
        rows = pl.ds(pl.multiple_of(lax.rem(x + r, NX) * TOK + start, 128), size)
        second = ref[...]
        second_ref[rows, :] = second
        z = nn(second, wu_s[...]) + bias_ref[0:1, :]
        sq = z * z
        t = jnp.tanh(k0 * z * (1.0 + k1 * sq))
        half = 0.5 * (1.0 + t)
        act_ref[rows, :] = (z * half).astype(bf16)
        slope = half + 0.5 * z * (1.0 - t * t) * (k0 * (1.0 + 3.0 * k1 * sq))
        gb = (slope * nt(grad_ref[rows, :], wd_ref[...])).astype(bf16)
        gb_ref[rows, :] = gb
        bias = bias + jnp.sum(gb.astype(f32), axis=0, keepdims=True)
        back_ref[...] = nt(gb, wu_s[...]).astype(bf16)
    sum_ref[0:1, :] = bias


def grad_qkv_kernel(pos_ref, normed_t_ref, own_ref, come_ref, keep_ref, send_ref, sum_ref):
    core = pos_ref[2]
    ones = jnp.ones((8, NX * TOK), bf16)
    for half, ref in ((0, own_ref), (1, come_ref)):
        cols = slice(half * 384, half * 384 + 384)
        sum_ref[:, cols] = nn(ones, ref[...])
        for n in range(8):
            part = nn(normed_t_ref[128 * n : 128 * n + 128, :], ref[...]).astype(bf16)
            first, second = part[:64], part[64:]
            keep_ref[n // 2, n % 2, :, cols] = jnp.where(core == 0, first, second)
            send_ref[n // 2, n % 2, :, cols] = jnp.where(core == 0, second, first)


def grad_normed_kernel(
    pos_ref, own_ref, come_ref, w_ref, unit_ref, p0_ref, p1_ref, far_lo_ref, far_hi_ref, p3_ref, sum_ref
):
    x = pos_ref[0]
    gain = jnp.zeros((1, D), f32)
    shift = jnp.zeros((1, D), f32)
    for r in range(NX):
        rows = pl.ds(pl.multiple_of(lax.rem(x + r, NX) * TOK, TOK), TOK)
        part = nt(own_ref[rows, :], w_ref[:, 0:384]) + nt(come_ref[rows, :], w_ref[:, 384:768])
        gain = gain + jnp.sum(part * unit_ref[rows, :].astype(f32), axis=0, keepdims=True)
        shift = shift + jnp.sum(part, axis=0, keepdims=True)
        low = part.astype(bf16)
        if r == 2:
            far_lo_ref[...] = low[:128]
            far_hi_ref[...] = low[128:]
        else:
            (p0_ref, p1_ref, None, p3_ref)[r][...] = low
    sum_ref[0:1, :] = gain
    sum_ref[1:2, :] = shift


def finish_ffn_kernel(pos_ref, all_ref, up_ref, down_ref):
    x = pos_ref[0]
    for n in range(NX):
        cols = pl.ds(pl.multiple_of(lax.rem(x - n + NX, NX) * D, D), D)
        for part in range(8):
            rows = slice(part * 16, part * 16 + 16)
            up_ref[rows, cols] = all_ref[part, n].astype(f32)
            down_ref[n * 128 + part * 16 : n * 128 + part * 16 + 16, :] = all_ref[part, 4 + n].astype(f32)


def finish_last_kernel(pos_ref, mine_ref, come_ref, qkv_ref, out_ref):
    x, zl, core, y = pos_ref[0], pos_ref[1], pos_ref[2], pos_ref[3]
    for ref, side in ((mine_ref, core), (come_ref, 1 - core)):
        for r in range(NY):
            rows = pl.ds(pl.multiple_of(side * 64 + lax.rem(y + r, NY) * 16, 16), 16)
            for n in range(NX):
                block = ref[r, n].astype(f32)
                out_ref[rows, 256 * n : 256 * n + 256] = block[:, 768:1024]
                base = lax.rem(x - n + NX, NX) * 256
                for half, pair in ((0, zl), (1, 1 - zl)):
                    for c in range(3):
                        cols = pl.ds(pl.multiple_of(c * D + base + pair * 128, 128), 128)
                        qkv_ref[rows, cols] = block[:, half * 384 + c * 128 : half * 384 + c * 128 + 128]


def place(zh, y, c, x, zl):
    return ((zh * NY + y) * 2 + c) * 8 + x * NZ + zl


def take_from(array, dx=0, dz=0, dy=0, dc=0, dh=0, flip_y=0):
    pairs = []
    for zh in range(2):
        for y in range(NY):
            for c in range(2):
                for x in range(NX):
                    for zl in range(NZ):
                        src = place((zh + dh) % 2, ((y ^ flip_y) + dy) % NY, (c + dc) % 2, (x + dx) % NX, (zl + dz) % NZ)
                        pairs.append((src, place(zh, y, c, x, zl)))
    return lax.ppermute(array, ("replica", "shard"), pairs)


def piece(array, index, size, axis):
    return lax.dynamic_slice_in_dim(array, index * size, size, axis)


def put(target, value, index, axis):
    starts = [0] * target.ndim
    starts[axis] = index
    return lax.dynamic_update_slice(target, value.astype(target.dtype), starts)


def from_partner(array, axis, core):
    half = array.shape[axis] // 2
    mine = take_from(piece(array, core, half, axis), dz=1)
    other = take_from(mine, dc=1)
    out = jnp.zeros_like(array)
    return put(put(out, mine, core * half, axis), other, (1 - core) * half, axis)


def add_low(*parts):
    total = parts[0].astype(f32)
    for part in parts[1:]:
        total = total + part.astype(f32)
    return total.astype(bf16)


Y_CORE = [[(zh * NY + y) * 2 + c for y in range(NY) for c in range(2)] for zh in range(2)]
X_RING = [[x * NZ + zl for x in range(NX)] for zl in range(NZ)]


def spread_x(parts):
    return [parts[0]] + [take_from(parts[r], dx=-r) for r in range(1, NX)]


def ring_gather(block):
    half = block.shape[0] // 2
    up = take_from(block, dx=1)
    down = take_from(block, dx=-1)
    return [block, up, take_from(up[:half], dx=1), take_from(down[half:], dx=-1), down]


def ring_sum(own, next_one, far_lo, far_hi, last):
    return ring_sum_end(own, next_one, *ring_sum_begin(far_lo, far_hi), last)


def ring_sum_begin(far_lo, far_hi):
    return take_from(far_lo, dx=-1), take_from(far_hi, dx=1)


def ring_sum_end(own, next_one, low, high, last):
    half = low.shape[0]
    up = jnp.concatenate([add_low(next_one[:half], low), next_one[half:]])
    down = jnp.concatenate([last[:half], add_low(last[half:], high)])
    return own.astype(f32) + take_from(up, dx=-1).astype(f32) + take_from(down, dx=1).astype(f32)


def after(values, *marks):
    return lax.optimization_barrier((values, marks))[0]


def normalize(values):
    center = values - jnp.mean(values, axis=-1, keepdims=True)
    spread = jnp.mean(center * center, axis=-1, keepdims=True)
    return center * lax.rsqrt(spread + 1e-05)


def layer_norm(values, gain, shift):
    return normalize(values) * gain + shift


def reduce_core(array, core):
    return add_low(piece(array, core, 64, 2), take_from(piece(array, 1 - core, 64, 2), dc=1))


def reduce_y(held, y):
    come = [take_from(piece(held, (y + r) % NY, 16, 2), dy=-r) for r in range(1, NY)]
    return add_low(piece(held, y, 16, 2), *come)


def reduce_z(held, zl, flip=None):
    own = jnp.squeeze(piece(held, zl, 1, 1), 1)
    other = jnp.squeeze(piece(held, 1 - zl, 1, 1), 1)
    if flip is not None:
        other = flip(other)
    near = own.astype(f32) + take_from(other, dz=1).astype(f32)
    far = take_from(own, dh=1).astype(f32) + take_from(other, dz=1, dh=1).astype(f32)
    return (near + far).astype(bf16)


def to_owner_x(part, x):
    return jnp.concatenate(spread_x([lax.dynamic_index_in_dim(part, (x + r) % NX, 0) for r in range(NX)]))


def gather_y(part):
    return jnp.stack([part] + [take_from(part, dy=r) for r in range(1, NY)])


def total(parts):
    return functools.reduce(jnp.add, [p.astype(f32) for p in parts])


def slope_table():
    table = np.zeros((8, 8, 128), np.float32)
    for s in range(8):
        for h in range(2):
            rest = SLOPES[2 * s + h]
            for n in range(3):
                part = np.float32(np.asarray(rest).astype(jnp.bfloat16))
                rest = np.float32(rest - part)
                table[s, :, 64 * (1 - h) + n] = part
                table[s, :, 64 * (1 - h) + 3 + n] = part
    return table


def per_device(hidden_in, segments, out_grad, w_qkv, w_out, w_up, w_down, norm_gains, bias_rows, up_bias):
    replica = lax.axis_index("replica")
    shard = lax.axis_index("shard")
    core = replica % 2
    y = (replica // 2) % NY
    x = shard // NZ
    zl = shard % NZ

    pack = jnp.concatenate(
        [
            norm_gains,
            bias_rows,
            up_bias.reshape(4, 128),
            segments.astype(bf16).reshape(2, 128),
            jnp.zeros((2, 128), bf16),
        ]
    )
    pos = jnp.stack([x, zl, core, y]).astype(jnp.int32)
    pack_near = take_from(pack, dz=1)
    pair = jnp.concatenate([pack, pack_near])
    pairs = [pair] + [take_from(pair, dx=r) for r in range(1, NX)]
    packs = [part[16 * n : 16 * n + 16] for part in pairs for n in range(2)]
    wide, up_row, seg_rows = call(
        wide_kernel, [((16, D), f32), ((8, D), f32), ((16, 128), f32)], "small_arrays", pos, *packs
    )
    gains = wide[0:2]
    biases = wide[2:8]
    seg_col = seg_rows.reshape(SEQ, 1)

    send = call(pick_kernel, [((128, 768), bf16)] * NX, "pick_qkv", pos, w_qkv)
    come = spread_x(send)
    hidden_b = after(hidden_in, send)
    ring_up = take_from(hidden_b, dx=1)
    ring_down = take_from(hidden_b, dx=-1)
    ring_lo = take_from(ring_up[:128], dx=1)
    ring_hi = take_from(ring_down[128:], dx=-1)
    up_near = take_from(after(piece(w_up, core, 64, 0), send), dz=1)
    come_b = after(come, wide, up_near)
    half = jnp.stack([piece(part, core, 64, 0) for part in come_b])
    near = take_from(jnp.concatenate([half[..., 384:], half[..., :384]], axis=-1), dz=1)
    cross = take_from(near, dc=1)

    out_half = piece(after(w_out, send), core, 512, 1)
    out_near = take_from(out_half, dz=1)
    out_pair = jnp.where(zl == 0, jnp.concatenate([out_half, out_near]), jnp.concatenate([out_near, out_half]))
    out_mine = lax.all_gather(
        after(out_pair, near), "shard", axis=0, axis_index_groups=X_RING, tiled=True
    )


    def qkv_bias(pair):
        parts = [lax.dynamic_slice(biases[n], (x * 256 + pair * 128,), (128,)) for n in (1, 2)]
        return jnp.concatenate([parts[0], jnp.zeros((128,), f32), parts[1]])

    first_rows = jnp.stack([gains[0], biases[0]])
    mixed_other, normed_all, unit_all, qkv_x = call(
        first_kernel,
        [((NX * TOK, 384), bf16), ((NX * TOK, D), bf16), ((NX * TOK, D), bf16), ((D, 768), bf16)],
        "first_norm_qkv",
        pos,
        hidden_in,
        ring_up,
        ring_down,
        ring_lo,
        ring_hi,
        first_rows,
        qkv_bias(1 - zl)[None],
        *come,
        near,
        cross,
        flops=7 * 10**9,
    )
    mixed_come = take_from(mixed_other, dz=1)
    mixed_own = (nn(normed_all, qkv_x[:, :384]) + qkv_bias(zl)).astype(bf16)

    grad_all = lax.all_gather(
        after(out_grad, mixed_other), "shard", axis=0, axis_index_groups=X_RING, tiled=True
    )
    send = call(pick_up_kernel, [((192, D), bf16)] * NX, "pick_up", after(pos, mixed_other), w_up, up_near)
    come = spread_x(send)
    out_cross = take_from(after(out_mine, mixed_come), dc=1)
    normed_t = after(normed_all, mixed_other).T
    mixed_come = after(mixed_come, normed_t, come)

    slopes = lax.dynamic_index_in_dim(jnp.asarray(slope_table()), shard, 0, keepdims=False)
    ctx_f, ctx_low, queries_back = attn_fwd(pos, mixed_own, mixed_come, seg_col, slopes)
    context = lax.all_to_all(ctx_low.reshape(8, TOK, 128), "shard", 0, 0)
    context = context.transpose(1, 0, 2).reshape(TOK, D)

    out_mine, out_cross = after((out_mine, out_cross), ctx_low)
    out_left = jnp.where(core == 0, out_mine, out_cross)
    out_right = jnp.where(core == 0, out_cross, out_mine)

    rows_in = hidden_in.astype(f32)
    middle = rows_in + jnp.concatenate([nn(context, out_left), nn(context, out_right)], axis=1) + biases[3]
    second_f, second_pull = jax.vjp(layer_norm, middle, gains[1], biases[4])
    second = second_f.astype(bf16)

    down_near = take_from(after(piece(w_down, core, 256, 0), context), dz=1)
    down_cross = take_from(down_near, dc=1)
    up_cross = take_from(jnp.stack([part[128:192] for part in after(come, ctx_low)]), dc=1)
    ring = ring_gather(second)
    full = ((NX * TOK, D), bf16)
    *back, second_all, act, grad_before, grad_bias_up, down_x = call(
        ffn_kernel,
        [((TOK, D), bf16), ((TOK, D), bf16), ((128, D), bf16), ((128, D), bf16), ((TOK, D), bf16)]
        + [full, full, full, ((8, D), f32), full],
        "feed_forward",
        pos,
        ring[0],
        ring[1],
        ring[4],
        ring[2],
        ring[3],
        grad_all,
        up_row,
        *come,
        up_cross,
        w_down,
        down_near,
        down_cross,
        scratch=[pltpu.VMEM((D, D), bf16)],
        flops=17 * 10**9,
    )
    grad_bias_up = grad_bias_up[0]
    low, high = ring_sum_begin(back[2], back[3])
    grad_second = ring_sum_end(back[0], back[1], low, high, back[4])

    second_all, act = after((second_all, act), low, high)
    grad_up = tn(second_all, grad_before).astype(bf16).reshape(NX, NZ, 128, D)
    grad_down = tn(act, grad_all).astype(bf16).reshape(NZ, NX, 128, D)
    ffn_parts = jnp.concatenate([grad_up, grad_down.transpose(1, 0, 2, 3)]).reshape(8, NZ, 8, 16, D)
    ffn_parts = after(ffn_parts, grad_second)
    ffn_y = lax.psum_scatter(
        ffn_parts.transpose(2, 0, 1, 3, 4).reshape(-1, D),
        "replica",
        scatter_dimension=0,
        axis_index_groups=Y_CORE,
        tiled=True,
    ).reshape(8, NZ, 16, D)

    upstream = out_grad.astype(f32)
    grad_bias_down = jnp.sum(upstream, axis=0)
    grad_mid_norm, grad_gain_two, grad_shift_two = second_pull(grad_second)
    grad_middle = upstream + grad_mid_norm
    grad_branch = grad_middle.astype(bf16)
    grad_bias_out = jnp.sum(grad_branch.astype(f32), axis=0)
    grad_context = (nt(grad_branch[:, :512], out_left) + nt(grad_branch[:, 512:], out_right)).astype(bf16)
    grad_ctx = lax.all_to_all(grad_context.reshape(TOK, 8, 128), "shard", 1, 0).reshape(SEQ, 128)

    ahead = nn(act, after(down_x, grad_second)).astype(bf16)
    down_sum = lax.psum_scatter(
        after(ahead, grad_ctx), "shard", scatter_dimension=0, axis_index_groups=X_RING, tiled=True
    )
    grad_out = tn(context, grad_branch).astype(bf16).reshape(NX, NZ, 128, D)
    out_held = reduce_core(grad_out, core)
    d_own, d_other = attn_bwd(pos, queries_back, mixed_own, mixed_come, grad_ctx, ctx_f, seg_col)
    d_own, d_other = after((d_own, d_other), out_held)

    d_come = take_from(d_other, dz=1)
    out_held = after(out_held, d_other)
    out_parts = spread_x([lax.dynamic_index_in_dim(out_held, (x + r) % NX, 0, keepdims=False) for r in range(NX)])
    out_sum = add_low(*out_parts)
    ffn_z = reduce_z(after(ffn_y, d_come), zl)

    qkv_keep, qkv_send, sums = call(
        grad_qkv_kernel,
        [((NX, NZ, 64, 768), bf16), ((NX, NZ, 64, 768), bf16), ((8, 768), f32)],
        "grad_qkv",
        pos,
        normed_t,
        d_own,
        d_come,
        flops=7 * 10**9,
    )
    qkv_held = add_low(qkv_keep, take_from(qkv_send, dc=1))
    *low, first_sums = call(
        grad_normed_kernel,
        [((TOK, D), bf16), ((TOK, D), bf16), ((128, D), bf16), ((128, D), bf16), ((TOK, D), bf16), ((8, D), f32)],
        "grad_normed",
        after(pos, sums),
        d_own,
        d_come,
        qkv_x,
        unit_all,
        flops=7 * 10**9,
    )
    grad_gain_one, grad_shift_one = first_sums[0], first_sums[1]
    sums_own, sums_come = sums[0, :384], sums[0, 384:]

    def wide_row(n):
        row = jnp.zeros((D,), f32)
        row = lax.dynamic_update_slice(row, sums_own[128 * n : 128 * n + 128], (x * 256 + zl * 128,))
        return lax.dynamic_update_slice(row, sums_come[128 * n : 128 * n + 128], (x * 256 + (1 - zl) * 128,))

    rows = jnp.stack(
        [
            grad_gain_one,
            grad_gain_two,
            grad_shift_one,
            wide_row(0),
            wide_row(2),
            grad_bias_out,
            grad_shift_two,
            grad_bias_down,
        ]
    )
    up_wide = lax.dynamic_update_slice(jnp.zeros((4 * D,), f32), grad_bias_up, (x * D,))
    small = jnp.concatenate(
        [rows.reshape(8, 8, 128).transpose(1, 0, 2), up_wide.reshape(8, 4, 128), jnp.zeros((8, 4, 128), f32)], axis=1
    )
    small = jnp.sum(lax.all_to_all(small, "shard", 0, 0), axis=0)

    low_come, high_come = ring_sum_begin(low[2], low[3])
    low_come, high_come, qkv_held, ffn_z = lax.optimization_barrier((low_come, high_come, qkv_held, ffn_z))
    ffn_x = to_owner_x(ffn_z[:4], x)
    grad_normed = ring_sum_end(low[0], low[1], low_come, high_come, low[4])
    out_side = jnp.stack([out_sum[..., 256 * n : 256 * n + 256] for n in range(4)])
    last_y = reduce_y(jnp.concatenate([qkv_held, out_side], axis=-1), y)
    small_core = take_from(small, dc=1)
    grad_normed, last_y, ffn_x, small_core = lax.optimization_barrier((grad_normed, last_y, ffn_x, small_core))
    small = small + small_core
    _, first_pull = jax.vjp(lambda rows: layer_norm(rows, gains[0], biases[0]), rows_in)
    in_grad = grad_middle + first_pull(grad_normed)[0]
    hidden_out = (middle + after(down_sum, first_sums).astype(f32) + biases[5]).astype(bf16)

    ffn_part = jnp.concatenate([ffn_x, ffn_z[4:]])
    final_up, final_down = call(
        finish_ffn_kernel,
        [((128, 4 * D), f32), ((512, D), f32)],
        "finish_ffn",
        pos,
        lax.all_gather(ffn_part, "replica", axis=0, axis_index_groups=Y_CORE),
    )

    turn = lambda part: jnp.concatenate([part[..., 384:768], part[..., :384], part[..., 768:]], axis=-1)
    last_z, small_y = lax.optimization_barrier((reduce_z(last_y, zl, turn), take_from(small, flip_y=1)))
    small = small + small_y
    last_x = to_owner_x(last_z[..., :768], x)
    last_x, small_y = lax.optimization_barrier((last_x, take_from(small, dy=2)))
    small = small + small_y
    last_part = gather_y(jnp.concatenate([last_x, last_z[..., 768:]], axis=-1))
    last_part, small_h = lax.optimization_barrier((last_part, take_from(small, dh=1)))
    small = small + small_h
    final_qkv, final_out = call(
        finish_last_kernel,
        [((128, 3 * D), f32), ((128, D), f32)],
        "finish_qkv",
        pos,
        last_part,
        take_from(last_part, dc=1),
    )

    return (
        hidden_out,
        in_grad,
        final_qkv,
        final_out,
        final_up,
        final_down,
        small[0:2],
        small[2:8],
        small[8:12].reshape(512),
    )


def solution(mesh):
    return jax.shard_map(
        per_device,
        mesh=mesh,
        in_specs=(
            P(("replica", "shard"), None),
            P(("replica", "shard")),
            P(("replica", "shard"), None),
            P("shard", None),
            P("shard", None),
            P("shard", None),
            P("shard", None),
            P(None, "shard"),
            P(None, "shard"),
            P("shard"),
        ),
        out_specs=(
            P(("replica", "shard"), None),
            P(("replica", "shard"), None),
            P("shard", None),
            P("shard", None),
            P("shard", None),
            P("shard", None),
            P(None, "shard"),
            P(None, "shard"),
            P("shard"),
        ),
        check_vma=False,
    )
```

```python
import functools

import jax
import jax.numpy as jnp
import numpy as np
from jax import lax
from jax.experimental import pallas as pl
from jax.experimental.pallas import tpu as pltpu
from jax.sharding import PartitionSpec as P

f32 = jnp.float32
bf16 = jnp.bfloat16

D = 1024
H = 16
HD = 64
TOK = 256
SEQ = 2048
NX, NZ, NY = 4, 2, 4
FWD_ROWS = 1024
BWD_ROWS = 512
FAR = -1e30
VMEM_BYTES = 60 * 2**20

SLOPES = (2.0 ** (-8.0 * (np.arange(H) + 1) / H) / 128).astype(np.float32)


def nt(a, b):
    return lax.dot_general(a, b, (((1,), (1,)), ((), ())), preferred_element_type=f32)


def nn(a, b):
    return lax.dot_general(a, b, (((1,), (0,)), ((), ())), preferred_element_type=f32)


def tn(a, b):
    return lax.dot_general(a, b, (((0,), (0,)), ((), ())), preferred_element_type=f32)


def pieces(x):
    a = x.astype(bf16).astype(f32)
    r = x - a
    b = r.astype(bf16).astype(f32)
    return a, b, r - b


def lane_of(rows):
    return lax.broadcasted_iota(jnp.int32, (rows, 128), 1)


def key_features(seg_col, rows):
    feat = lane_of(rows) & 63
    pos = lax.broadcasted_iota(jnp.int32, (rows, 128), 0)
    coarse = (pos & -256).astype(f32)
    fine = (pos & 255).astype(f32)
    flag = (seg_col.astype(f32) == (feat - 9).astype(f32)).astype(f32)
    out = jnp.where(feat < 3, coarse, jnp.where(feat < 6, fine, jnp.where(feat < 9, 1.0, flag)))
    return jnp.where(feat < 14, out, 0.0).astype(bf16)


def join_rows(pos_ref, own_ref, come_ref, out_ref):
    zl = pos_ref[1]
    for n in range(NX):
        rows = pl.ds(n * TOK, TOK)
        for ref, side in ((own_ref, zl), (come_ref, 1 - zl)):
            out_ref[pl.ds(pl.multiple_of((2 * n + side) * TOK, TOK), TOK), :] = ref[rows, :]


def fwd_kernel(bq, pos_ref, own_ref, come_ref, seg_ref, segq_ref, slope_ref, c_ref, low_ref, qb_ref, h_s, k_s, vt_s, q_s):
    i = pl.program_id(0)

    @pl.when(i == 0)
    def _():
        join_rows(pos_ref, own_ref, come_ref, h_s)
        k_ref = h_s.at[:, 128:256]
        v_ref = h_s.at[:, 256:384]
        feats = key_features(seg_ref[...], SEQ)
        left = lane_of(SEQ) < 64
        k_s[0] = jnp.where(left, k_ref[...], feats)
        k_s[1] = jnp.where(left, feats, k_ref[...])
        vt = v_ref[...].T
        for h in range(2):
            vt_s[h, 0:64, :] = vt[64 * h : 64 * h + 64]
            vt_s[h, 64:80, :] = jnp.ones((16, SEQ), bf16)

    lane = lane_of(bq)
    feat = lane & 63
    left = lane < 64
    off = jnp.where(segq_ref[...].astype(f32) == (feat - 9).astype(f32), 0.0, FAR)
    base = jnp.where(feat < 9, slope_ref[0:1, :], jnp.where(feat < 14, off, 0.0))
    q = h_s[pl.ds(pl.multiple_of(i * bq, bq), bq), 0:128].astype(f32) * (HD**-0.5)
    q_s[0] = jnp.where(left, q, base).astype(bf16)
    q_s[1] = jnp.where(left, base, q).astype(bf16)

    def tile(j, carry, diag):
        out = []
        for h in range(2):
            top, acc = carry[h]
            s = nt(k_s[h, pl.ds(pl.multiple_of(j * bq, bq), bq), :], q_s[h])
            if diag:
                kk = lax.broadcasted_iota(jnp.int32, (bq, bq), 0)
                qq = lax.broadcasted_iota(jnp.int32, (bq, bq), 1)
                s = jnp.where(kk <= qq, s, FAR)
            new = jnp.maximum(top, jnp.max(s, axis=0, keepdims=True))
            p = jnp.exp(s - new).astype(bf16)
            o = nn(vt_s[h, :, pl.ds(pl.multiple_of(j * bq, bq), bq)], p)
            out.append((new, acc * jnp.exp(top - new) + o))
        return tuple(out)

    init = tuple((jnp.full((1, bq), FAR, f32), jnp.zeros((80, bq), f32)) for _ in range(2))
    carry = tile(i, init, True)
    carry = lax.fori_loop(0, i, lambda j, c: tile(j, c, False), carry)
    outs = []
    rows = lax.broadcasted_iota(jnp.int32, (128, bq), 0)
    spread = jnp.zeros((128, bq), f32)
    for h in range(2):
        top, acc = carry[h]
        total = acc[64:65]
        outs.append(acc[:64] / total)
        for n, part in enumerate(pieces(-(top + jnp.log(total)))):
            spread = jnp.where(rows == 64 * (1 - h) + 6 + n, part, spread)
    ctx = jnp.concatenate(outs, axis=0).T
    c_ref[...] = ctx
    low_ref[...] = ctx.astype(bf16)
    full = base + spread.T
    qb_ref[0] = jnp.where(left, q, full).astype(bf16)
    qb_ref[1] = jnp.where(left, full, q).astype(bf16)


def attn_fwd(pos, own, come, seg_col, slopes):
    bq = FWD_ROWS
    whole = pl.BlockSpec((SEQ // 2, 384), lambda i: (0, 0))
    block = pl.BlockSpec((bq, 128), lambda i: (i, 0))
    return pl.pallas_call(
        functools.partial(fwd_kernel, bq),
        grid=(SEQ // bq,),
        in_specs=[
            pl.BlockSpec(memory_space=pltpu.SMEM),
            whole,
            whole,
            pl.BlockSpec((SEQ, 1), lambda i: (0, 0)),
            pl.BlockSpec((bq, 1), lambda i: (i, 0)),
            pl.BlockSpec((8, 128), lambda i: (0, 0)),
        ],
        out_specs=[block, block, pl.BlockSpec((2, bq, 128), lambda i: (0, i, 0))],
        out_shape=[
            jax.ShapeDtypeStruct((SEQ, 128), f32),
            jax.ShapeDtypeStruct((SEQ, 128), bf16),
            jax.ShapeDtypeStruct((2, SEQ, 128), bf16),
        ],
        scratch_shapes=[
            pltpu.VMEM((SEQ, 384), bf16),
            pltpu.VMEM((2, SEQ, 128), bf16),
            pltpu.VMEM((2, 80, SEQ), bf16),
            pltpu.VMEM((2, bq, 128), bf16),
        ],
        compiler_params=pltpu.CompilerParams(vmem_limit_bytes=VMEM_BYTES),
        cost_estimate=pl.CostEstimate(flops=14 * 10**9, bytes_accessed=4 * 2**20, transcendentals=5 * 10**6),
        name="attn_fwd",
    )(pos, own, come, seg_col, seg_col, slopes)


def bwd_kernel(
    bq, pos_ref, q_ref, own_ref, come_ref, d_ref, c_ref, seg_ref, mine_ref, other_ref, h_s, out_ref, k_s, v_s, kt_s, d_s, dk_acc, dv_acc
):
    i = pl.program_id(0)
    n = pl.num_programs(0)

    @pl.when(i == 0)
    def _():
        join_rows(pos_ref, own_ref, come_ref, h_s)
        k_ref = h_s.at[:, 128:256]
        v_ref = h_s.at[:, 256:384]
        feats = key_features(seg_ref[...], SEQ)
        left = lane_of(SEQ) < 64
        k_s[0] = jnp.where(left, k_ref[...], feats)
        k_s[1] = jnp.where(left, feats, k_ref[...])
        v_s[0] = jnp.where(left, v_ref[...], feats)
        v_s[1] = jnp.where(left, feats, v_ref[...])
        kt_s[...] = k_ref[...].T

    lane = lane_of(bq)
    feat = lane & 63
    left = lane < 64
    grad = d_ref[...].astype(f32)
    prod = grad * c_ref[...]
    for h in range(2):
        mine = left if h == 0 else ~left
        a, b, c = pieces(-jnp.sum(jnp.where(mine, prod, 0.0), axis=1, keepdims=True))
        extra = jnp.where(feat == 6, a, jnp.where(feat == 7, b, jnp.where(feat == 8, c, 0.0)))
        d_s[h] = jnp.where(mine, grad, extra).astype(bf16)

    def tile(j, carry, diag):
        out = []
        rows = pl.ds(pl.multiple_of(j * bq, bq), bq)
        for h in range(2):
            s = nt(k_s[h, rows, :], q_ref[h])
            if diag:
                kk = lax.broadcasted_iota(jnp.int32, (bq, bq), 0)
                qq = lax.broadcasted_iota(jnp.int32, (bq, bq), 1)
                s = jnp.where(kk <= qq, s, FAR)
            p = jnp.exp(s)
            ds = (p * nt(v_s[h, rows, :], d_s[h])).astype(bf16)
            dv = nn(p.astype(bf16), d_s[h])
            dk = nn(ds, q_ref[h])
            if diag:
                dv_acc[h, rows, :] = dv
                dk_acc[h, rows, :] = dk
            else:
                dv_acc[h, rows, :] += dv
                dk_acc[h, rows, :] += dk
            out.append(carry[h] + nn(kt_s[64 * h : 64 * h + 64, rows], ds))
        return tuple(out)

    init = tuple(jnp.zeros((64, bq), f32) for _ in range(2))
    carry = tile(i, init, True)
    carry = lax.fori_loop(0, i, lambda j, c: tile(j, c, False), carry)
    dq = (jnp.concatenate(carry, axis=0) * (HD**-0.5)).T
    out_ref[pl.ds(pl.multiple_of(i * bq, bq), bq), 0:128] = dq.astype(bf16)

    @pl.when(i == n - 1)
    def _():
        side = lane_of(SEQ) < 64
        out_ref[:, 128:256] = jnp.where(side, dk_acc[0], dk_acc[1]).astype(bf16)
        out_ref[:, 256:384] = jnp.where(side, dv_acc[0], dv_acc[1]).astype(bf16)
        zl = pos_ref[1]
        for m in range(NX):
            rows = pl.ds(m * TOK, TOK)
            mine_ref[rows, :] = out_ref[pl.ds(pl.multiple_of((2 * m + zl) * TOK, TOK), TOK), :]
            other_ref[rows, :] = out_ref[pl.ds(pl.multiple_of((2 * m + 1 - zl) * TOK, TOK), TOK), :]


def attn_bwd(pos, qb, own, come, d, ctx, seg_col):
    bq = BWD_ROWS
    whole = pl.BlockSpec((SEQ // 2, 384), lambda i: (0, 0))
    block = pl.BlockSpec((bq, 128), lambda i: (i, 0))
    return pl.pallas_call(
        functools.partial(bwd_kernel, bq),
        grid=(SEQ // bq,),
        in_specs=[
            pl.BlockSpec(memory_space=pltpu.SMEM),
            pl.BlockSpec((2, bq, 128), lambda i: (0, i, 0)),
            whole,
            whole,
            block,
            block,
            pl.BlockSpec((SEQ, 1), lambda i: (0, 0)),
        ],
        out_specs=[whole, whole],
        out_shape=[jax.ShapeDtypeStruct((SEQ // 2, 384), bf16)] * 2,
        scratch_shapes=[
            pltpu.VMEM((SEQ, 384), bf16),
            pltpu.VMEM((SEQ, 384), bf16),
            pltpu.VMEM((2, SEQ, 128), bf16),
            pltpu.VMEM((2, SEQ, 128), bf16),
            pltpu.VMEM((128, SEQ), bf16),
            pltpu.VMEM((2, bq, 128), bf16),
            pltpu.VMEM((2, SEQ, 128), f32),
            pltpu.VMEM((2, SEQ, 128), f32),
        ],
        compiler_params=pltpu.CompilerParams(vmem_limit_bytes=VMEM_BYTES),
        cost_estimate=pl.CostEstimate(flops=23 * 10**9, bytes_accessed=6 * 2**20, transcendentals=5 * 10**6),
        name="attn_bwd",
    )(pos, qb, own, come, d, ctx, seg_col)


def call(kernel, outs, name, *args, scratch=(), flops=10**9):
    smem = pl.BlockSpec(memory_space=pltpu.SMEM)
    vmem = pl.BlockSpec(memory_space=pltpu.VMEM)
    return pl.pallas_call(
        kernel,
        in_specs=[smem] + [vmem] * (len(args) - 1),
        out_specs=[vmem] * len(outs),
        out_shape=[jax.ShapeDtypeStruct(shape, dtype) for shape, dtype in outs],
        scratch_shapes=scratch,
        cost_estimate=pl.CostEstimate(flops=flops, bytes_accessed=2**20, transcendentals=0),
        compiler_params=pltpu.CompilerParams(vmem_limit_bytes=VMEM_BYTES),
        name=name,
    )(*args)


def wide_kernel(pos_ref, *refs):
    *parts, wide_ref, up_ref, seg_ref = refs
    x, zl = pos_ref[0], pos_ref[1]
    for r in range(NX):
        for side, start in ((zl, 0), (1 - zl, 128)):
            part = parts[r][128:144, start : start + 128].astype(f32)
            owner = 2 * lax.rem(x - r + NX, NX) + side
            wide_ref[:, pl.ds(pl.multiple_of(owner * 128, 128), 128)] = part
            seg_ref[pl.ds(pl.multiple_of(owner * 2, 2), 2), :] = part[12:14, :]
            if r == 0:
                for n in range(4):
                    cols = pl.ds(pl.multiple_of(side * 512 + n * 128, 128), 128)
                    up_ref[0:1, cols] = part[8 + n : 9 + n, :]


def pick_kernel(pos_ref, w_ref, pack_ref, near_ref, *out_refs):
    x, zl = pos_ref[0], pos_ref[1]
    for r in range(NX):
        dest = lax.rem(x + r, NX)
        out_refs[r][128:144, 0:128] = pack_ref[...]
        out_refs[r][128:144, 128:256] = near_ref[...]
        out_refs[r][128:144, 256:768] = jnp.zeros((16, 512), bf16)
        for half, pair in ((0, zl), (1, 1 - zl)):
            for c in range(3):
                start = pl.multiple_of(c * D + dest * 256 + pair * 128, 128)
                out_refs[r][0:128, half * 384 + c * 128 : half * 384 + c * 128 + 128] = w_ref[:, pl.ds(start, 128)]


def pick_up_kernel(pos_ref, w_ref, near_ref, *out_refs):
    for r in range(NX):
        start = pl.multiple_of(lax.rem(pos_ref[0] + r, NX) * D, D)
        out_refs[r][0:128, :] = w_ref[:, pl.ds(start, D)]
        out_refs[r][128:192, :] = near_ref[:, pl.ds(start, D)]


def first_kernel(
    pos_ref, own_ref, up_ref, down_ref, far_lo_ref, far_hi_ref, rows_ref, bias_ref, w0_ref, w1_ref, w2_ref, w3_ref,
    near_ref, cross_ref, other_ref, normed_ref, unit_ref, w_ref,
):
    x, zl, core = pos_ref[0], pos_ref[1], pos_ref[2]
    for r, ref in enumerate((w0_ref, w1_ref, w2_ref, w3_ref)):
        come = lax.rem(x - r + NX, NX)
        w_ref[pl.ds(pl.multiple_of((2 * come + zl) * 128, 128), 128), :] = ref[0:128, :]
        base = (2 * come + 1 - zl) * 128
        for part, side in ((near_ref, core), (cross_ref, 1 - core)):
            rows = pl.ds(pl.multiple_of(base + side * 64, 64), 64)
            w_ref[rows, :] = part[r]
    blocks = ((own_ref, 0, 0, 256), (up_ref, 1, 0, 256), (far_lo_ref, 2, 0, 128), (far_hi_ref, 2, 128, 128), (down_ref, 3, 0, 256))
    for ref, r, start, size in blocks:
        values = ref[...].astype(f32)
        center = values - jnp.mean(values, axis=-1, keepdims=True)
        spread = jnp.mean(center * center, axis=-1, keepdims=True)
        unit = center * lax.rsqrt(spread + 1e-05)
        normed = (unit * rows_ref[0:1, :] + rows_ref[1:2, :]).astype(bf16)
        rows = pl.ds(pl.multiple_of(lax.rem(x + r, NX) * TOK + start, 128), size)
        normed_ref[rows, :] = normed
        unit_ref[rows, :] = unit.astype(bf16)
        other_ref[rows, :] = (nn(normed, w_ref[:, 384:768]) + bias_ref[0:1, :]).astype(bf16)


def ffn_kernel(
    pos_ref, own_ref, up_ref, down_ref, far_lo_ref, far_hi_ref, grad_ref, bias_ref, u0_ref, u1_ref, u2_ref, u3_ref,
    ucross_ref, d_ref, dnear_ref, dcross_ref,
    p0_ref, p1_ref, plo_ref, phi_ref, p3_ref, second_ref, act_ref, gb_ref, sum_ref, wd_ref, wu_s,
):
    x, zl, core = pos_ref[0], pos_ref[1], pos_ref[2]
    for r, ref in enumerate((u0_ref, u1_ref, u2_ref, u3_ref)):
        come = lax.rem(x - r + NX, NX)
        wu_s[pl.ds(pl.multiple_of((2 * come + zl) * 128, 128), 128), :] = ref[0:128, :]
        base = (2 * come + 1 - zl) * 128
        wu_s[pl.ds(pl.multiple_of(base + core * 64, 64), 64), :] = ref[128:192, :]
        wu_s[pl.ds(pl.multiple_of(base + (1 - core) * 64, 64), 64), :] = ucross_ref[r]
    wd_ref[pl.ds(pl.multiple_of(zl * 512, 512), 512), :] = d_ref[...]
    for part, side in ((dnear_ref, core), (dcross_ref, 1 - core)):
        wd_ref[pl.ds(pl.multiple_of((1 - zl) * 512 + side * 256, 256), 256), :] = part[...]
    blocks = (
        (own_ref, 0, 0, 256, p0_ref),
        (up_ref, 1, 0, 256, p1_ref),
        (down_ref, 3, 0, 256, p3_ref),
        (far_lo_ref, 2, 0, 128, plo_ref),
        (far_hi_ref, 2, 128, 128, phi_ref),
    )
    bias = jnp.zeros((1, D), f32)
    k0, k1 = np.float32(np.sqrt(2 / np.pi)), np.float32(0.044715)
    for ref, r, start, size, back_ref in blocks:
        rows = pl.ds(pl.multiple_of(lax.rem(x + r, NX) * TOK + start, 128), size)
        second = ref[...]
        second_ref[rows, :] = second
        z = nn(second, wu_s[...]) + bias_ref[0:1, :]
        sq = z * z
        t = jnp.tanh(k0 * z * (1.0 + k1 * sq))
        half = 0.5 * (1.0 + t)
        act_ref[rows, :] = (z * half).astype(bf16)
        slope = half + 0.5 * z * (1.0 - t * t) * (k0 * (1.0 + 3.0 * k1 * sq))
        gb = (slope * nt(grad_ref[rows, :], wd_ref[...])).astype(bf16)
        gb_ref[rows, :] = gb
        bias = bias + jnp.sum(gb.astype(f32), axis=0, keepdims=True)
        back_ref[...] = nt(gb, wu_s[...]).astype(bf16)
    sum_ref[0:1, :] = bias


def grad_qkv_kernel(pos_ref, normed_t_ref, own_ref, come_ref, keep_ref, send_ref, sum_ref):
    core = pos_ref[2]
    ones = jnp.ones((8, NX * TOK), bf16)
    for half, ref in ((0, own_ref), (1, come_ref)):
        cols = slice(half * 384, half * 384 + 384)
        sum_ref[:, cols] = nn(ones, ref[...])
        for n in range(8):
            part = nn(normed_t_ref[128 * n : 128 * n + 128, :], ref[...]).astype(bf16)
            first, second = part[:64], part[64:]
            keep_ref[n // 2, n % 2, :, cols] = jnp.where(core == 0, first, second)
            send_ref[n // 2, n % 2, :, cols] = jnp.where(core == 0, second, first)


def grad_normed_kernel(
    pos_ref, own_ref, come_ref, w_ref, unit_ref, p0_ref, p1_ref, far_lo_ref, far_hi_ref, p3_ref, sum_ref
):
    x = pos_ref[0]
    gain = jnp.zeros((1, D), f32)
    shift = jnp.zeros((1, D), f32)
    for r in range(NX):
        rows = pl.ds(pl.multiple_of(lax.rem(x + r, NX) * TOK, TOK), TOK)
        part = nt(own_ref[rows, :], w_ref[:, 0:384]) + nt(come_ref[rows, :], w_ref[:, 384:768])
        gain = gain + jnp.sum(part * unit_ref[rows, :].astype(f32), axis=0, keepdims=True)
        shift = shift + jnp.sum(part, axis=0, keepdims=True)
        low = part.astype(bf16)
        if r == 2:
            far_lo_ref[...] = low[:128]
            far_hi_ref[...] = low[128:]
        else:
            (p0_ref, p1_ref, None, p3_ref)[r][...] = low
    sum_ref[0:1, :] = gain
    sum_ref[1:2, :] = shift


def finish_ffn_kernel(pos_ref, all_ref, up_ref, down_ref):
    x = pos_ref[0]
    for n in range(NX):
        cols = pl.ds(pl.multiple_of(lax.rem(x - n + NX, NX) * D, D), D)
        for part in range(8):
            rows = slice(part * 16, part * 16 + 16)
            up_ref[rows, cols] = all_ref[part, n].astype(f32)
            down_ref[n * 128 + part * 16 : n * 128 + part * 16 + 16, :] = all_ref[part, 4 + n].astype(f32)


def finish_last_kernel(pos_ref, mine_ref, come_ref, qkv_ref, out_ref):
    x, zl, core, y = pos_ref[0], pos_ref[1], pos_ref[2], pos_ref[3]
    for ref, side in ((mine_ref, core), (come_ref, 1 - core)):
        for r in range(NY):
            rows = pl.ds(pl.multiple_of(side * 64 + lax.rem(y + r, NY) * 16, 16), 16)
            for n in range(NX):
                block = ref[r, n].astype(f32)
                out_ref[rows, 256 * n : 256 * n + 256] = block[:, 768:1024]
                base = lax.rem(x - n + NX, NX) * 256
                for half, pair in ((0, zl), (1, 1 - zl)):
                    for c in range(3):
                        cols = pl.ds(pl.multiple_of(c * D + base + pair * 128, 128), 128)
                        qkv_ref[rows, cols] = block[:, half * 384 + c * 128 : half * 384 + c * 128 + 128]


def place(zh, y, c, x, zl):
    return ((zh * NY + y) * 2 + c) * 8 + x * NZ + zl


def take_from(array, dx=0, dz=0, dy=0, dc=0, dh=0, flip_y=0):
    pairs = []
    for zh in range(2):
        for y in range(NY):
            for c in range(2):
                for x in range(NX):
                    for zl in range(NZ):
                        src = place((zh + dh) % 2, ((y ^ flip_y) + dy) % NY, (c + dc) % 2, (x + dx) % NX, (zl + dz) % NZ)
                        pairs.append((src, place(zh, y, c, x, zl)))
    return lax.ppermute(array, ("replica", "shard"), pairs)


def piece(array, index, size, axis):
    return lax.dynamic_slice_in_dim(array, index * size, size, axis)


def put(target, value, index, axis):
    starts = [0] * target.ndim
    starts[axis] = index
    return lax.dynamic_update_slice(target, value.astype(target.dtype), starts)


def from_partner(array, axis, core):
    half = array.shape[axis] // 2
    mine = take_from(piece(array, core, half, axis), dz=1)
    other = take_from(mine, dc=1)
    out = jnp.zeros_like(array)
    return put(put(out, mine, core * half, axis), other, (1 - core) * half, axis)


def add_low(*parts):
    total = parts[0].astype(f32)
    for part in parts[1:]:
        total = total + part.astype(f32)
    return total.astype(bf16)


Y_CORE = [[(zh * NY + y) * 2 + c for y in range(NY) for c in range(2)] for zh in range(2)]
X_RING = [[x * NZ + zl for x in range(NX)] for zl in range(NZ)]


def spread_x(parts):
    return [parts[0]] + [take_from(parts[r], dx=-r) for r in range(1, NX)]


def ring_gather(block):
    half = block.shape[0] // 2
    up = take_from(block, dx=1)
    down = take_from(block, dx=-1)
    return [block, up, take_from(up[:half], dx=1), take_from(down[half:], dx=-1), down]


def ring_sum(own, next_one, far_lo, far_hi, last):
    return ring_sum_end(own, next_one, *ring_sum_begin(far_lo, far_hi), last)


def ring_sum_begin(far_lo, far_hi):
    return take_from(far_lo, dx=-1), take_from(far_hi, dx=1)


def ring_sum_end(own, next_one, low, high, last):
    half = low.shape[0]
    up = jnp.concatenate([add_low(next_one[:half], low), next_one[half:]])
    down = jnp.concatenate([last[:half], add_low(last[half:], high)])
    return own.astype(f32) + take_from(up, dx=-1).astype(f32) + take_from(down, dx=1).astype(f32)


def after(values, *marks):
    return lax.optimization_barrier((values, marks))[0]


def normalize(values):
    center = values - jnp.mean(values, axis=-1, keepdims=True)
    spread = jnp.mean(center * center, axis=-1, keepdims=True)
    return center * lax.rsqrt(spread + 1e-05)


def layer_norm(values, gain, shift):
    return normalize(values) * gain + shift


def reduce_core(array, core):
    return add_low(piece(array, core, 64, 2), take_from(piece(array, 1 - core, 64, 2), dc=1))


def reduce_y(held, y):
    come = [take_from(piece(held, (y + r) % NY, 16, 2), dy=-r) for r in range(1, NY)]
    return add_low(piece(held, y, 16, 2), *come)


def reduce_z(held, zl, flip=None):
    own = jnp.squeeze(piece(held, zl, 1, 1), 1)
    other = jnp.squeeze(piece(held, 1 - zl, 1, 1), 1)
    if flip is not None:
        other = flip(other)
    near = own.astype(f32) + take_from(other, dz=1).astype(f32)
    far = take_from(own, dh=1).astype(f32) + take_from(other, dz=1, dh=1).astype(f32)
    return (near + far).astype(bf16)


def to_owner_x(part, x):
    return jnp.concatenate(spread_x([lax.dynamic_index_in_dim(part, (x + r) % NX, 0) for r in range(NX)]))


def gather_y(part):
    return jnp.stack([part] + [take_from(part, dy=r) for r in range(1, NY)])


def total(parts):
    return functools.reduce(jnp.add, [p.astype(f32) for p in parts])


def slope_table():
    table = np.zeros((8, 8, 128), np.float32)
    for s in range(8):
        for h in range(2):
            rest = SLOPES[2 * s + h]
            for n in range(3):
                part = np.float32(np.asarray(rest).astype(jnp.bfloat16))
                rest = np.float32(rest - part)
                table[s, :, 64 * (1 - h) + n] = part
                table[s, :, 64 * (1 - h) + 3 + n] = part
    return table


def per_device(hidden_in, segments, out_grad, w_qkv, w_out, w_up, w_down, norm_gains, bias_rows, up_bias):
    replica = lax.axis_index("replica")
    shard = lax.axis_index("shard")
    core = replica % 2
    y = (replica // 2) % NY
    x = shard // NZ
    zl = shard % NZ

    pack = jnp.concatenate(
        [
            norm_gains,
            bias_rows,
            up_bias.reshape(4, 128),
            segments.astype(bf16).reshape(2, 128),
            jnp.zeros((2, 128), bf16),
        ]
    )
    pos = jnp.stack([x, zl, core, y]).astype(jnp.int32)
    pack_near = take_from(pack, dz=1)

    send = call(pick_kernel, [((144, 768), bf16)] * NX, "pick_qkv", pos, w_qkv, pack, pack_near)
    come = spread_x(send)
    ring_up = take_from(hidden_in, dx=1)
    ring_down = take_from(hidden_in, dx=-1)
    up_near = take_from(piece(w_up, core, 64, 0), dz=1)
    come, ring_up, ring_down, up_near = lax.optimization_barrier((come, ring_up, ring_down, up_near))
    ring_lo = take_from(ring_up[:128], dx=1)
    ring_hi = take_from(ring_down[128:], dx=-1)
    wide, up_row, seg_rows = call(
        wide_kernel, [((16, D), f32), ((8, D), f32), ((16, 128), f32)], "small_arrays", pos, *come
    )
    gains = wide[0:2]
    biases = wide[2:8]
    seg_col = seg_rows.reshape(SEQ, 1)
    half = jnp.stack([piece(part[:128], core, 64, 0) for part in come])
    near = take_from(jnp.concatenate([half[..., 384:], half[..., :384]], axis=-1), dz=1)
    near, ring_lo, ring_hi = lax.optimization_barrier((near, ring_lo, ring_hi))
    cross = take_from(near, dc=1)

    out_half = piece(after(w_out, send), core, 512, 1)
    out_near = take_from(out_half, dz=1)
    out_pair = jnp.where(zl == 0, jnp.concatenate([out_half, out_near]), jnp.concatenate([out_near, out_half]))
    out_mine = lax.all_gather(
        after(out_pair, near), "shard", axis=0, axis_index_groups=X_RING, tiled=True
    )


    def qkv_bias(pair):
        parts = [lax.dynamic_slice(biases[n], (x * 256 + pair * 128,), (128,)) for n in (1, 2)]
        return jnp.concatenate([parts[0], jnp.zeros((128,), f32), parts[1]])

    first_rows = jnp.stack([gains[0], biases[0]])
    mixed_other, normed_all, unit_all, qkv_x = call(
        first_kernel,
        [((NX * TOK, 384), bf16), ((NX * TOK, D), bf16), ((NX * TOK, D), bf16), ((D, 768), bf16)],
        "first_norm_qkv",
        pos,
        hidden_in,
        ring_up,
        ring_down,
        ring_lo,
        ring_hi,
        first_rows,
        qkv_bias(1 - zl)[None],
        *come,
        near,
        cross,
        flops=7 * 10**9,
    )
    mixed_come = take_from(mixed_other, dz=1)
    mixed_own = (nn(normed_all, qkv_x[:, :384]) + qkv_bias(zl)).astype(bf16)

    send = call(pick_up_kernel, [((192, D), bf16)] * NX, "pick_up", after(pos, mixed_other), w_up, up_near)
    come = spread_x(send)
    grad_all = lax.all_gather(after(out_grad, mixed_other), "shard", axis=0, axis_index_groups=X_RING, tiled=True)
    out_cross = take_from(after(out_mine, mixed_come), dc=1)
    normed_t = after(normed_all, mixed_other).T
    mixed_come = after(mixed_come, normed_t)

    slopes = lax.dynamic_index_in_dim(jnp.asarray(slope_table()), shard, 0, keepdims=False)
    ctx_f, ctx_low, queries_back = attn_fwd(pos, mixed_own, mixed_come, seg_col, slopes)
    ctx_low = after(ctx_low, come)
    context = lax.all_to_all(ctx_low.reshape(8, TOK, 128), "shard", 0, 0)
    context = context.transpose(1, 0, 2).reshape(TOK, D)

    out_mine, out_cross = after((out_mine, out_cross), ctx_low)
    out_left = jnp.where(core == 0, out_mine, out_cross)
    out_right = jnp.where(core == 0, out_cross, out_mine)

    rows_in = hidden_in.astype(f32)
    middle = rows_in + jnp.concatenate([nn(context, out_left), nn(context, out_right)], axis=1) + biases[3]
    second_f, second_pull = jax.vjp(layer_norm, middle, gains[1], biases[4])
    second = second_f.astype(bf16)

    down_near = take_from(after(piece(w_down, core, 256, 0), context), dz=1)
    down_cross = take_from(down_near, dc=1)
    up_cross = take_from(jnp.stack([part[128:192] for part in after(come, ctx_low)]), dc=1)
    ring = ring_gather(second)
    full = ((NX * TOK, D), bf16)
    *back, second_all, act, grad_before, grad_bias_up, down_x = call(
        ffn_kernel,
        [((TOK, D), bf16), ((TOK, D), bf16), ((128, D), bf16), ((128, D), bf16), ((TOK, D), bf16)]
        + [full, full, full, ((8, D), f32), full],
        "feed_forward",
        pos,
        ring[0],
        ring[1],
        ring[4],
        ring[2],
        ring[3],
        grad_all,
        up_row,
        *come,
        up_cross,
        w_down,
        down_near,
        down_cross,
        scratch=[pltpu.VMEM((D, D), bf16)],
        flops=17 * 10**9,
    )
    grad_bias_up = grad_bias_up[0]
    low, high = ring_sum_begin(back[2], back[3])
    grad_second = ring_sum_end(back[0], back[1], low, high, back[4])

    second_all, act = after((second_all, act), low, high)
    grad_up = tn(second_all, grad_before).astype(bf16).reshape(NX, NZ, 128, D)
    grad_down = tn(act, grad_all).astype(bf16).reshape(NZ, NX, 128, D)
    ffn_parts = jnp.concatenate([grad_up, grad_down.transpose(1, 0, 2, 3)]).reshape(8, NZ, 8, 16, D)
    ffn_parts = after(ffn_parts, grad_second)
    ffn_y = lax.psum_scatter(
        ffn_parts.transpose(2, 0, 1, 3, 4).reshape(-1, D),
        "replica",
        scatter_dimension=0,
        axis_index_groups=Y_CORE,
        tiled=True,
    ).reshape(8, NZ, 16, D)

    upstream = out_grad.astype(f32)
    grad_bias_down = jnp.sum(upstream, axis=0)
    grad_mid_norm, grad_gain_two, grad_shift_two = second_pull(grad_second)
    grad_middle = upstream + grad_mid_norm
    grad_branch = grad_middle.astype(bf16)
    grad_bias_out = jnp.sum(grad_branch.astype(f32), axis=0)
    grad_context = (nt(grad_branch[:, :512], out_left) + nt(grad_branch[:, 512:], out_right)).astype(bf16)
    grad_ctx = lax.all_to_all(grad_context.reshape(TOK, 8, 128), "shard", 1, 0).reshape(SEQ, 128)

    ahead = nn(act, after(down_x, grad_second)).astype(bf16)
    down_sum = lax.psum_scatter(
        after(ahead, grad_ctx), "shard", scatter_dimension=0, axis_index_groups=X_RING, tiled=True
    )
    grad_out = tn(context, grad_branch).astype(bf16).reshape(NX, NZ, 128, D)
    out_held = reduce_core(grad_out, core)
    d_own, d_other = attn_bwd(pos, queries_back, mixed_own, mixed_come, grad_ctx, ctx_f, seg_col)
    d_own, d_other = after((d_own, d_other), out_held)

    d_come = take_from(d_other, dz=1)
    out_held = after(out_held, d_other)
    out_parts = spread_x([lax.dynamic_index_in_dim(out_held, (x + r) % NX, 0, keepdims=False) for r in range(NX)])
    out_sum = add_low(*out_parts)
    ffn_z = reduce_z(after(ffn_y, d_come), zl)

    qkv_keep, qkv_send, sums = call(
        grad_qkv_kernel,
        [((NX, NZ, 64, 768), bf16), ((NX, NZ, 64, 768), bf16), ((8, 768), f32)],
        "grad_qkv",
        pos,
        normed_t,
        d_own,
        d_come,
        flops=7 * 10**9,
    )
    qkv_held = add_low(qkv_keep, take_from(qkv_send, dc=1))
    *low, first_sums = call(
        grad_normed_kernel,
        [((TOK, D), bf16), ((TOK, D), bf16), ((128, D), bf16), ((128, D), bf16), ((TOK, D), bf16), ((8, D), f32)],
        "grad_normed",
        after(pos, sums),
        d_own,
        d_come,
        qkv_x,
        unit_all,
        flops=7 * 10**9,
    )
    grad_gain_one, grad_shift_one = first_sums[0], first_sums[1]
    sums_own, sums_come = sums[0, :384], sums[0, 384:]

    def wide_row(n):
        row = jnp.zeros((D,), f32)
        row = lax.dynamic_update_slice(row, sums_own[128 * n : 128 * n + 128], (x * 256 + zl * 128,))
        return lax.dynamic_update_slice(row, sums_come[128 * n : 128 * n + 128], (x * 256 + (1 - zl) * 128,))

    rows = jnp.stack(
        [
            grad_gain_one,
            grad_gain_two,
            grad_shift_one,
            wide_row(0),
            wide_row(2),
            grad_bias_out,
            grad_shift_two,
            grad_bias_down,
        ]
    )
    up_wide = lax.dynamic_update_slice(jnp.zeros((4 * D,), f32), grad_bias_up, (x * D,))
    small = jnp.concatenate(
        [rows.reshape(8, 8, 128).transpose(1, 0, 2), up_wide.reshape(8, 4, 128), jnp.zeros((8, 4, 128), f32)], axis=1
    )
    small = jnp.sum(lax.all_to_all(small, "shard", 0, 0), axis=0)

    low_come, high_come = ring_sum_begin(low[2], low[3])
    low_come, high_come, qkv_held, ffn_z = lax.optimization_barrier((low_come, high_come, qkv_held, ffn_z))
    ffn_x = to_owner_x(ffn_z[:4], x)
    grad_normed = ring_sum_end(low[0], low[1], low_come, high_come, low[4])
    out_side = jnp.stack([out_sum[..., 256 * n : 256 * n + 256] for n in range(4)])
    last_y = reduce_y(jnp.concatenate([qkv_held, out_side], axis=-1), y)
    small_core = take_from(small, dc=1)
    grad_normed, last_y, ffn_x, small_core = lax.optimization_barrier((grad_normed, last_y, ffn_x, small_core))
    small = small + small_core
    _, first_pull = jax.vjp(lambda rows: layer_norm(rows, gains[0], biases[0]), rows_in)
    in_grad = grad_middle + first_pull(grad_normed)[0]
    hidden_out = (middle + after(down_sum, first_sums).astype(f32) + biases[5]).astype(bf16)

    ffn_part = jnp.concatenate([ffn_x, ffn_z[4:]])
    final_up, final_down = call(
        finish_ffn_kernel,
        [((128, 4 * D), f32), ((512, D), f32)],
        "finish_ffn",
        pos,
        lax.all_gather(ffn_part, "replica", axis=0, axis_index_groups=Y_CORE),
    )

    turn = lambda part: jnp.concatenate([part[..., 384:768], part[..., :384], part[..., 768:]], axis=-1)
    last_z, small_y = lax.optimization_barrier((reduce_z(last_y, zl, turn), take_from(small, flip_y=1)))
    small = small + small_y
    last_x = to_owner_x(last_z[..., :768], x)
    last_x, small_y = lax.optimization_barrier((last_x, take_from(small, dy=2)))
    small = small + small_y
    last_part = gather_y(jnp.concatenate([last_x, last_z[..., 768:]], axis=-1))
    last_part, small_h = lax.optimization_barrier((last_part, take_from(small, dh=1)))
    small = small + small_h
    final_qkv, final_out = call(
        finish_last_kernel,
        [((128, 3 * D), f32), ((128, D), f32)],
        "finish_qkv",
        pos,
        last_part,
        take_from(last_part, dc=1),
    )

    return (
        hidden_out,
        in_grad,
        final_qkv,
        final_out,
        final_up,
        final_down,
        small[0:2],
        small[2:8],
        small[8:12].reshape(512),
    )


def solution(mesh):
    return jax.shard_map(
        per_device,
        mesh=mesh,
        in_specs=(
            P(("replica", "shard"), None),
            P(("replica", "shard")),
            P(("replica", "shard"), None),
            P("shard", None),
            P("shard", None),
            P("shard", None),
            P("shard", None),
            P(None, "shard"),
            P(None, "shard"),
            P("shard"),
        ),
        out_specs=(
            P(("replica", "shard"), None),
            P(("replica", "shard"), None),
            P("shard", None),
            P("shard", None),
            P("shard", None),
            P("shard", None),
            P(None, "shard"),
            P(None, "shard"),
            P("shard"),
        ),
        check_vma=False,
    )
```
